512 devices in a mesh: team: 8 (over y_hi, core), blk: 64 (over z, x, y_lo).
Axes of the slice: x: 4, y: 8 (y_hi: 4, y_lo: 2; y = y_hi * 2 + y_lo), z: 8, core: 2. Of those that a mesh axis runs over, the one named last changes fastest.
Arguments:
- xdata: bfloat16 [2048, 131072], P('team', 'blk'), may hold values from -6 to 6
- omega_tiles: bfloat16 [64, 32, 256, 256], P('blk', 'team'), may hold values from -2 to 3, as said below
- tile_rows: int32 [64, 32], P('blk'), may hold values from 0 to 511, as said below
- tile_cols: int32 [64, 32], P('blk'), may hold values from 0 to 511, as said below
Outputs:
- updated_tiles: bfloat16 [64, 32, 256, 256], P('blk', 'team')
The draws below stay inside these ranges and needn't reach their ends.
Inputs may be any that keep to these rules, and one draw needn't show every extreme that they name: Each index b of blk owns 8 block-rows, each block-row has one owner, and slots 0 to 7 of b hold its block-rows' diagonal tiles (tile_rows = tile_cols); every other slot of b belongs to one of these block-rows. `tile_cols`: within one owner, no two slots name block-columns c with the same c // 8, so one owner needs at most one panel from each index of blk, and needs exactly 32 of them. `omega_tiles`: the diagonal entries of diagonal tiles lie in 1 to 3.
All inputs are finite; a program needn't handle non-finite values.
Results may differ from the reference program's by a relative error of at most 0.017.
Values may be sent and summed in bfloat16 or wider, within the bound.
A program may use at most 128 MiB of HBM per device.

```python
import jax
import jax.numpy as jnp
from jax import lax

TILE = 256
ROWS_DEV = 8
NS_T = 256
NB = 512
P_SIZE = 131072
SLOTS = 32
NS = 2048
N_TEAM = 8
N_BLK = 64


def layout_pair(key):
    shifts = jax.random.permutation(jax.random.fold_in(key, 11), N_BLK)[:ROWS_DEV]
    extra = SLOTS - ROWS_DEV

    def per_device(device):
        dev_key = jax.random.fold_in(key, 100 + device)
        home_devices = (device - shifts) % N_BLK
        owned_rows = home_devices * ROWS_DEV + jnp.arange(ROWS_DEV, dtype=jnp.int32)
        ranking = jax.random.permutation(jax.random.fold_in(dev_key, 1), N_BLK)
        taken_peer = jnp.any(jnp.arange(N_BLK)[:, None] == home_devices[None, :], axis=1)
        ranked_keys = ranking + taken_peer.astype(jnp.int32) * N_BLK
        chosen = jnp.argsort(ranked_keys)[:extra]
        sub_index = jax.random.randint(jax.random.fold_in(dev_key, 2), (extra,), 0, ROWS_DEV)
        which_row = jax.random.randint(jax.random.fold_in(dev_key, 3), (extra,), 0, ROWS_DEV)
        slot_rows = jnp.concatenate([owned_rows, owned_rows[which_row]])
        slot_cols = jnp.concatenate([owned_rows, (chosen * ROWS_DEV + sub_index).astype(jnp.int32)])
        return (slot_rows.astype(jnp.int32), slot_cols.astype(jnp.int32))
    return jax.vmap(per_device)(jnp.arange(N_BLK, dtype=jnp.int32))


def draw_tile_rows(key, part):
    return layout_pair(key)[0]


def draw_tile_cols(key, part):
    return layout_pair(key)[1]


def draw_omega_tiles(key, part):
    key = jax.random.fold_in(key, 5)
    shape = (N_BLK, SLOTS, TILE, TILE)
    values = jnp.clip(0.3 * jax.random.normal(jax.random.fold_in(key, 1), shape, jnp.float32), -1.8, 1.8)
    diagonal = jnp.exp(jax.random.uniform(jax.random.fold_in(key, 3), shape, jnp.float32, 0.0, jnp.log(3.0)))
    slot_ids = jnp.arange(SLOTS)[None, :, None, None]
    entry_a = jnp.arange(TILE)[None, None, :, None]
    entry_b = jnp.arange(TILE)[None, None, None, :]
    mask = (slot_ids < ROWS_DEV) & (entry_a == entry_b)
    return jnp.where(mask, diagonal, values).astype(jnp.bfloat16)


def block_levels(own_key, shape, shards, low, high):
    def one(position, parts):
        draws = jax.random.uniform(jax.random.fold_in(jax.random.fold_in(own_key, 6), position), (parts,), jnp.float32, low / len(shards), high / len(shards))
        return jnp.repeat(jnp.exp(draws), shape[position] // parts).reshape((-1,) + (1,) * (len(shape) - position - 1))

    gain = one(*shards[0])
    for cut in shards[1:]:
        gain = gain * one(*cut)
    return gain


def normal_values(stream_key, shape, deviation, most, shards=(), held_as=jnp.bfloat16):
    values = jax.random.normal(stream_key, shape, jnp.float32) * deviation
    if len(shards) > 0:
        values = block_levels(stream_key, shape, shards, -0.22, 0.18) * values
    return jnp.clip(values, min=-most, max=most).astype(held_as)


def setup_inputs(seed: int = 0) -> dict:
    keys = jax.random.split(jax.random.key(seed), 5)
    xdata = normal_values(keys[0], (NS, P_SIZE), 1.0, 6.0, ((0, 8), (1, 64)))
    omega_tiles = draw_omega_tiles(jax.random.fold_in(keys[4], 71), 0)
    tile_rows = draw_tile_rows(jax.random.fold_in(keys[4], 71), 0)
    tile_cols = draw_tile_cols(jax.random.fold_in(keys[4], 71), 0)
    return {"xdata": xdata, "omega_tiles": omega_tiles, "tile_rows": tile_rows, "tile_cols": tile_cols}


def reference(xdata, omega_tiles, tile_rows, tile_cols):
    grouped = xdata.reshape(N_TEAM, NS_T, NB, TILE)
    ident = jnp.eye(TILE, dtype=jnp.float32)

    def per_device(items):
        omega_dev, slot_rows, slot_cols = items
        panels = grouped[:, :, slot_cols, :].astype(jnp.float32)
        products = jnp.einsum('sab,tnsb->tsan', omega_dev.astype(jnp.float32), panels, precision=lax.Precision.HIGHEST)
        same_row = (slot_rows[:, None] == slot_rows[None, :]).astype(jnp.float32)
        row_products = jnp.einsum('rs,tsan->tran', same_row, products, precision=lax.Precision.HIGHEST).astype(jnp.bfloat16)
        partials = jnp.einsum('tran,tnrb->trab', row_products.astype(jnp.float32), panels, precision=lax.Precision.HIGHEST).astype(jnp.bfloat16)
        summed = jnp.sum(partials.astype(jnp.float32), axis=0)
        own_tiles = omega_dev.astype(jnp.float32)
        diag_mask = (slot_rows == slot_cols)[:, None, None] & (ident[None, :, :] > 0.5)
        inverse = jnp.where(diag_mask, 1.0 / jnp.where(diag_mask, own_tiles, 1.0), 0.0)
        gradient = summed / NS - inverse
        stepped = own_tiles - 0.5 * gradient
        shrunk = jnp.sign(stepped) * jnp.maximum(jnp.abs(stepped) - 0.05, 0.0)
        return jnp.where(diag_mask, stepped, shrunk).astype(jnp.bfloat16)

    return lax.map(per_device, (omega_tiles, tile_rows, tile_cols))
```

```python
import jax
import jax.numpy as jnp
from jax import lax
from jax.experimental import pallas as pl
from jax.experimental.pallas import tpu as pltpu
from jax.sharding import PartitionSpec as P

MESH = pl.DeviceIdType.MESH
NZ, NX, NH = 8, 4, 4
TILE = 256
SLOTS = 32
CHUNKS = 4
ROWS = TILE // CHUNKS
UNITS = NZ * CHUNKS
LAG_Y = 3
LAG_R = 5
OM_STEP = 12

HERE, Y_XM, Y_X2, Y_XP, Y_ME, XP_OWN, XP_RELAY, XP_PAIR, XM_OWN, XM_PAIR, XM_RELAY, X2_OWN, X2_PAIR = range(13)


def kernel(x_ref, om_ref, rows_v, cols_v, rows_s, cols_s, out_ref,
           zb, stgx, ystg, rec, om, yb, acc, gx, grx, gown, hs, relr, fs, fr, wq, wsm, tsm,
           zs, zsh, zr, ss, ys_r, rp_r, rm_r, ends, wsend, wrecv, oms, omr, ocs, ocr, gs, gr, hss, hsr, fss, fsr, loc):
    t = lax.axis_index("team")
    b = lax.axis_index("blk")
    core, yh = t % 2, t // 2
    z, x, y = b // 8, (b // 2) % 4, b % 2

    def plane(dx, f):
        yy = 1 - y if f else y
        return (t, z * 8 + ((x + dx) % NX) * 2 + yy)

    zp = (t, ((z + 1) % NZ) * 8 + b % 8)
    zm = (t, ((z + NZ - 1) % NZ) * 8 + b % 8)
    xp, xm, yq = plane(1, 0), plane(3, 0), plane(0, 1)
    cq = (yh * 2 + 1 - core, b)
    hp = (((yh + 1) % NH) * 2 + core, b)
    hm = (((yh + 3) % NH) * 2 + core, b)

    def remote(src, dst, ssem, rsem, dev):
        return pltpu.make_async_remote_copy(src_ref=src, dst_ref=dst, send_sem=ssem, recv_sem=rsem,
                                            device_id=dev, device_id_type=MESH)

    loads = [pltpu.make_async_copy(x_ref.at[pl.ds(c * ROWS, ROWS), pl.ds(j * TILE, TILE)], zb.at[0, c, j], loc.at[c, j])
             for c in range(CHUNKS) for j in range(8)]
    for copy in loads:
        copy.start()
    om_load = pltpu.make_async_copy(om_ref.at[0], om.at[0, core], loc.at[CHUNKS, 0])
    om_load.start()

    partners = [zp, zm, cq, hp, hm] + [plane(dx, f) for dx in range(NX) for f in range(2) if dx or f]
    barrier = pltpu.get_barrier_semaphore()
    for dev in partners:
        pl.semaphore_signal(barrier, inc=1, device_id=dev, device_id_type=MESH)

    i0 = lax.broadcasted_iota(jnp.int32, (SLOTS, SLOTS), 0)
    i1 = lax.broadcasted_iota(jnp.int32, (SLOTS, SLOTS), 1)
    eye = i0 == i1
    rb = jnp.broadcast_to(rows_v[...], (SLOTS, SLOTS))
    cb = jnp.broadcast_to(cols_v[...], (SLOTS, SLOTS))
    rc = jnp.broadcast_to(jnp.sum(jnp.where(eye, rb, 0), axis=1, keepdims=True), (SLOTS, SLOTS))
    cc = jnp.sum(jnp.where(eye, cb, 0), axis=1, keepdims=True)
    rank = jnp.sum(jnp.where((rb < rc) | ((rb == rc) & (i1 < i0)), 1, 0), axis=1, keepdims=True)
    order = jnp.sum(jnp.where(rank == i1, i0, 0), axis=0, keepdims=True)
    last = jnp.sum(jnp.where(rc <= rb, 1, 0), axis=0, keepdims=True) - 1
    lane = lax.broadcasted_iota(jnp.int32, (SLOTS, 128), 1)
    ccw = jnp.broadcast_to(cc, (SLOTS, 128))
    wanted = jnp.sum(jnp.where((ccw >> 3) == lane, ccw & 7, 0), axis=0, keepdims=True)
    wq[0] = jnp.broadcast_to(wanted, (8, 128))
    tsm_v = wq.at[8]
    tsm_v[0:1, 0:SLOTS] = order
    tsm_v[1:2, 0:SLOTS] = last

    pl.semaphore_wait(barrier, len(partners))

    def w_copy(dx, f):
        place = dx * 2 + f
        return remote(wq.at[0], wq.at[place], wsend.at[place], wrecv.at[place], plane(dx, f))

    others = [(dx, f) for dx in range(NX) for f in range(2) if dx or f]
    for dx, f in others:
        w_copy(dx, f).start()
    t_copy = pltpu.make_async_copy(wq.at[8], tsm, loc.at[CHUNKS, 1])
    t_copy.start()

    def z_copy(d, k, c):
        if d == 0:
            sem = zs.at[0]
            return remote(zb.at[k - 1, c], zb.at[k, c], sem, zr.at[0, k, c], zp)
        return remote(zb.at[(9 - k) % 8, c], zb.at[8 - k, c], zs.at[1], zr.at[1, k, c], zm)

    def z_half(d, c):
        if d == 0:
            return remote(zb.at[3, c], zb.at[4, c], zsh.at[0], zr.at[0, 4, c], zp)
        return remote(zb.at[5, c], zb.at[4, c], zsh.at[1], zr.at[1, 4, c], zm)

    def rows(c):
        return pl.ds(pl.multiple_of(c * ROWS, ROWS), ROWS)

    def y_copy(k, c):
        return remote(ystg.at[k, c], rec.at[k, pl.ds(Y_XM, 4), rows(c)], ss.at[0], ys_r.at[k, c], yq)

    def own_up(k, c):
        return remote(stgx.at[k, c, pl.ds(0, 2)], rec.at[k, pl.ds(XP_OWN, 2), rows(c)], ss.at[1], rp_r.at[k, c], xp)

    def own_down(k, c):
        return remote(stgx.at[k, c, 2], rec.at[k, XM_OWN, rows(c)], ss.at[2], ends.at[0], xm)

    def pair_up(k, c):
        return remote(rec.at[k, Y_XP, rows(c)], rec.at[k, XP_PAIR, rows(c)], ss.at[3], ends.at[1], xp)

    def pair_down(k, c):
        return remote(rec.at[k, pl.ds(Y_XM, 2), rows(c)], rec.at[k, pl.ds(XM_PAIR, 2), rows(c)], ss.at[4], rm_r.at[k, c], xm)

    def relay_up(k, c):
        return remote(rec.at[k, XP_RELAY, rows(c)], rec.at[k, X2_OWN, rows(c)], ss.at[5], ends.at[2], xp)

    def relay_down(k, c):
        return remote(rec.at[k, XM_RELAY, rows(c)], rec.at[k, X2_PAIR, rows(c)], ss.at[6], ends.at[3], xm)

    def pick(k, c):
        holder = ((z - k + NZ) % NZ) * 8 + x * 2 + y
        for f in range(2):
            for e in range(NX):
                idx = wsm[((NX - e) % NX) * 2 + f, 0, holder]
                got = zb[k, c, 0]
                for j in range(1, 8):
                    got = jnp.where(idx == j, zb[k, c, j], got)
                if f == 1:
                    ystg[k, c, (3, 2, 1, 0)[e]] = got
                elif e == 0:
                    rec[k, HERE, rows(c)] = got
                else:
                    stgx[k, c, e - 1] = got
        y_copy(k, c).start()
        own_up(k, c).start()
        own_down(k, c).start()

    def unit(u):
        v = u - CHUNKS
        p, side = v // 2, v % 2
        d = p // CHUNKS + 1
        k = jnp.where(side == 0, d, 8 - d)
        c = p % CHUNKS
        far = v >= 6 * CHUNKS
        k = jnp.where(far, 4, k)
        c = jnp.where(far, (v - 6 * CHUNKS) // 2 + (CHUNKS // 2) * side, c)
        first = u < CHUNKS
        return jnp.where(first, 0, k), jnp.where(first, u, c), jnp.where(first, 0, d), side

    for c in range(CHUNKS):
        for j in range(8):
            loads[c * 8 + j].wait()
        z_copy(0, 1, c).start()
        z_copy(1, 1, c).start()

    om_load.wait()

    def om_copy(d, what):
        far = hp if d == 0 else hm
        if what == 0:
            return remote(om.at[0, core], om.at[1 if d == 0 else 3, core], oms.at[d], omr.at[d], far)
        half = pl.ds(0 if d == 0 else 2, 2)
        return remote(om.at[1 if d == 0 else 3, core, half], om.at[2, core, half], oms.at[2 + d], omr.at[2 + d], far)

    def om_core(g):
        return remote(om.at[g, core], om.at[g, core], ocs.at[g], ocr.at[g], cq)

    om_copy(0, 0).start()
    om_copy(1, 0).start()
    om_core(0).start()

    for dx, f in others:
        w_copy(dx, f).wait_recv()
    w_load = pltpu.make_async_copy(wq.at[pl.ds(0, 8)], wsm, loc.at[CHUNKS, 2])
    w_load.start()
    w_load.wait()

    for c in range(CHUNKS):
        pick(0, c)

    def y_step(u):
        k, c, _, _ = unit(u)
        y_copy(k, c).wait_recv()
        pair_up(k, c).start()
        pair_down(k, c).start()

    def up_step(u):
        k, c, _, _ = unit(u)
        own_up(k, c).wait_recv()
        relay_up(k, c).start()

    def down_step(u):
        k, c, _, _ = unit(u)
        pair_down(k, c).wait_recv()
        relay_down(k, c).start()

    def z_step(u):
        k, c, d, side = unit(u)

        @pl.when(side == 0)
        def _():
            z_copy(0, d, c).wait_recv()

            @pl.when(d < 3)
            def _():
                z_copy(0, d + 1, c).start()

            @pl.when((d == 3) & (c < CHUNKS // 2))
            def _():
                z_half(0, c).start()

        @pl.when(side == 1)
        def _():
            z_copy(1, d, c).wait_recv()

            @pl.when(d < 3)
            def _():
                z_copy(1, d + 1, c).start()

            @pl.when((d == 3) & (c >= CHUNKS // 2))
            def _():
                z_half(1, c).start()

        pick(k, c)

    def step(u, carry):
        @pl.when(u < UNITS)
        def _():
            z_step(u)

        @pl.when((u >= LAG_Y) & (u < UNITS + LAG_Y))
        def _():
            y_step(u - LAG_Y)
            up_step(u - LAG_Y)

        @pl.when(u >= LAG_R)
        def _():
            down_step(u - LAG_R)

        return carry

    def early(u, carry):
        y_step(u)
        up_step(u)
        return carry

    lax.fori_loop(0, CHUNKS - LAG_Y, early, 0)
    lax.fori_loop(CHUNKS, OM_STEP, step, 0)
    om_copy(0, 0).wait_recv()
    om_copy(0, 1).start()
    om_core(1).start()
    om_copy(1, 0).wait_recv()
    om_copy(1, 1).start()
    om_core(3).start()
    lax.fori_loop(OM_STEP, UNITS + LAG_R, step, 0)
    om_copy(0, 1).wait_recv()
    om_copy(1, 1).wait_recv()
    om_core(2).start()
    t_copy.wait()
    for g in (0, 1, 3, 2):
        om_core(g).wait_recv()
    whole = rec.at[:, HERE]
    for i in range(4):
        pltpu.make_async_copy(whole, whole, ends.at[i]).wait()

    def panel(s):
        h = cols_s[0, s] >> 3
        k = (z - (h >> 3) + NZ) & (NZ - 1)
        dx = (x - ((h >> 1) & 3) + NX) & (NX - 1)
        other = (h & 1) != y
        own = jnp.where(dx == 0, HERE, jnp.where(dx == 1, XP_OWN, jnp.where(dx == 2, X2_OWN, XM_OWN)))
        pair = jnp.where(dx == 0, Y_ME, jnp.where(dx == 1, XP_PAIR, jnp.where(dx == 2, X2_PAIR, XM_PAIR)))
        return rec[k, jnp.where(other, pair, own)]

    def row_step(i, before):
        s = tsm[0, i]
        row = rows_s[0, s]
        who = s >> 2
        tile = om[(yh - (who >> 1) + NH) & (NH - 1), who & 1, s & 3]
        prod = lax.dot_general(tile, panel(s), (((1,), (1,)), ((), ())), preferred_element_type=jnp.float32)
        total = jnp.where(row == before, acc[...], 0.0) + prod
        acc[...] = total
        yb[i] = total.astype(jnp.bfloat16)
        return row

    acc[...] = jnp.zeros_like(acc)
    lax.fori_loop(0, SLOTS, row_step, jnp.int32(-1))

    def grad(g, who, i):
        s = (((yh + g) % NH) * 2 + who) * 4 + i
        return jnp.dot(yb[tsm[1, s]], panel(s), preferred_element_type=jnp.float32)

    def for_pair(g):
        def one(i, carry):
            gx[g, i] = grad(g, 1 - core, i).astype(jnp.bfloat16)
            return carry

        lax.fori_loop(0, 4, one, 0)
        pair_copy(g).start()

    def for_me(g):
        def one(i, carry):
            gown[g, i] = grad(g, core, i)
            return carry

        lax.fori_loop(0, 4, one, 0)

    def pair_copy(g):
        return remote(gx.at[g], grx.at[g], gs.at[g], gr.at[g], cq)

    def half_copy(d):
        half = pl.ds(2 * d, 2)
        return remote(hs.at[half], relr.at[half], hss.at[d], hsr.at[d], hp if d == 0 else hm)

    def last_copy(d, h):
        half = pl.ds(2 * h, 2)
        return remote(fs.at[d, half], fr.at[d, half], fss.at[d, h], fsr.at[d, h], hp if d == 0 else hm)

    for_pair(2)
    for_pair(1)
    for_pair(3)
    for_me(2)
    pair_copy(2).wait_recv()
    hs[...] = (gown[2] + grx[2].astype(jnp.float32)).astype(jnp.bfloat16)
    half_copy(0).start()
    half_copy(1).start()
    for_me(1)
    for_me(3)
    for d, g in ((0, 1), (1, 3)):
        direct = 1 - d
        half = slice(2 * direct, 2 * direct + 2)
        pair_copy(g).wait_recv()
        fs[d, half] = (gown[g, half] + grx[g, half].astype(jnp.float32)).astype(jnp.bfloat16)
        last_copy(d, direct).start()
    for_pair(0)
    for_me(0)
    for d, g in ((0, 1), (1, 3)):
        half = slice(2 * d, 2 * d + 2)
        half_copy(d).wait_recv()
        fs[d, half] = (gown[g, half] + grx[g, half].astype(jnp.float32)
                       + relr[half].astype(jnp.float32)).astype(jnp.bfloat16)
        last_copy(d, d).start()
    pair_copy(0).wait_recv()
    for d in range(2):
        for h in range(2):
            last_copy(d, h).wait_recv()

    e0 = lax.broadcasted_iota(jnp.int32, (TILE, TILE), 0)
    e1 = lax.broadcasted_iota(jnp.int32, (TILE, TILE), 1)
    for i in range(4):
        s = t * 4 + i
        total = (gown[0, i] + grx[0, i].astype(jnp.float32)) + (fr[0, i].astype(jnp.float32) + fr[1, i].astype(jnp.float32))
        own = om[0, core, i].astype(jnp.float32)
        diag = jnp.where(rows_s[0, s] == cols_s[0, s], e0, -1) == e1
        inverse = jnp.where(diag, 1.0 / jnp.where(diag, own, 1.0), 0.0)
        stepped = own - 0.5 * (total / 2048.0 - inverse)
        shrunk = stepped - jnp.clip(stepped, -0.05, 0.05)
        out_ref[0, i] = jnp.where(diag, stepped, shrunk).astype(jnp.bfloat16)

    for dx, f in others:
        w_copy(dx, f).wait_send()
    for d in range(2):
        three = zb.at[pl.ds(0, 3)]
        pltpu.make_async_copy(three, three, zs.at[d]).wait()
        rest = zb.at[3, pl.ds(0, CHUNKS // 2)]
        pltpu.make_async_copy(rest, rest, zsh.at[d]).wait()
        om_copy(d, 0).wait_send()
        om_copy(d, 1).wait_send()
        half_copy(d).wait_send()
        for h in range(2):
            last_copy(d, h).wait_send()
    for g in range(4):
        om_core(g).wait_send()
        pair_copy(g).wait_send()
    for i, n in enumerate((4, 2, 1, 1, 2, 1, 1)):
        sent = rec.at[:, pl.ds(0, n)]
        pltpu.make_async_copy(sent, sent, ss.at[i]).wait()


def body(xdata, omega_tiles, tile_rows, tile_cols):
    bf, f32, i32 = jnp.bfloat16, jnp.float32, jnp.int32
    tile = (TILE, TILE)
    dma = pltpu.SemaphoreType.DMA
    vmem = pl.BlockSpec(memory_space=pltpu.VMEM)
    smem = pl.BlockSpec(memory_space=pltpu.SMEM)
    hbm = pl.BlockSpec(memory_space=pl.ANY)
    return pl.pallas_call(
        kernel,
        out_shape=jax.ShapeDtypeStruct(omega_tiles.shape, bf),
        in_specs=[hbm, hbm, vmem, vmem, smem, smem],
        out_specs=vmem,
        scratch_shapes=[
            pltpu.VMEM((NZ, CHUNKS, 8, ROWS, TILE), bf),
            pltpu.VMEM((NZ, CHUNKS, 3, ROWS, TILE), bf),
            pltpu.VMEM((NZ, CHUNKS, 4, ROWS, TILE), bf),
            pltpu.VMEM((NZ, 13) + tile, bf),
            pltpu.VMEM((NH, 2, 4) + tile, bf),
            pltpu.VMEM((SLOTS,) + tile, bf),
            pltpu.VMEM(tile, f32),
            pltpu.VMEM((NH, 4) + tile, bf),
            pltpu.VMEM((NH, 4) + tile, bf),
            pltpu.VMEM((NH, 4) + tile, f32),
            pltpu.VMEM((4,) + tile, bf),
            pltpu.VMEM((4,) + tile, bf),
            pltpu.VMEM((2, 4) + tile, bf),
            pltpu.VMEM((2, 4) + tile, bf),
            pltpu.VMEM((9, 8, 128), i32),
            pltpu.SMEM((8, 8, 128), i32),
            pltpu.SMEM((8, 128), i32),
            dma((2,)), dma((2,)), dma((2, 5, CHUNKS)),
            dma((7,)), dma((NZ, CHUNKS)), dma((NZ, CHUNKS)), dma((NZ, CHUNKS)), dma((4,)),
            dma((8,)), dma((8,)),
            dma((4,)), dma((4,)), dma((4,)), dma((4,)),
            dma((4,)), dma((4,)), dma((2,)), dma((2,)), dma((2, 2)), dma((2, 2)),
            dma((CHUNKS + 1, 8)),
        ],
        compiler_params=pltpu.CompilerParams(
            collective_id=0, has_side_effects=True, vmem_limit_bytes=60 * 1024 * 1024
        ),
    )(xdata, omega_tiles, tile_rows, tile_cols, tile_rows, tile_cols)


def solution(mesh):
    return jax.shard_map(
        body,
        mesh=mesh,
        in_specs=(P("team", "blk"), P("blk", "team", None, None), P("blk", None), P("blk", None)),
        out_specs=P("blk", "team", None, None),
        check_vma=False,
    )
```

```python
import jax
import jax.numpy as jnp
from jax import lax
from jax.experimental import pallas as pl
from jax.experimental.pallas import tpu as pltpu
from jax.sharding import PartitionSpec as P

MESH = pl.DeviceIdType.MESH
NZ, NX, NH = 8, 4, 4
TILE = 256
SLOTS = 32
CHUNKS = 4
ROWS = TILE // CHUNKS
NEAR = 3
UNITS = NZ * NEAR
LAG = 3
OM_STEP = 10

HERE, Y_XM, Y_X2, Y_XP, Y_ME, XP_OWN, XP_PAIR, XM_OWN, XM_PAIR, X2_OWN, X2_PAIR = range(11)


def kernel(x_ref, om_ref, rows_v, cols_v, rows_s, cols_s, out_ref,
           zb, z2, stgx, ystg, rec, om, yb, acc, gx, grx, gown, hs, relr, fs, fr, wq, wsm, tsm,
           zs, zsh, zr, z2s, z2h, z2r, gys, gyr, ss, ys_r, ends, wsend, wrecv, oms, omr, ocs, ocr, gs, gr, hss, hsr, fss, fsr, loc):
    t = lax.axis_index("team")
    b = lax.axis_index("blk")
    core, yh = t % 2, t // 2
    z, x, y = b // 8, (b // 2) % 4, b % 2

    def plane(dx, f):
        yy = 1 - y if f else y
        return (t, z * 8 + ((x + dx) % NX) * 2 + yy)

    zp = (t, ((z + 1) % NZ) * 8 + b % 8)
    zm = (t, ((z + NZ - 1) % NZ) * 8 + b % 8)
    xp, x2, xm, yq = plane(1, 0), plane(2, 0), plane(3, 0), plane(0, 1)
    cq = (yh * 2 + 1 - core, b)
    hp = (((yh + 1) % NH) * 2 + core, b)
    hm = (((yh + 3) % NH) * 2 + core, b)

    def remote(src, dst, ssem, rsem, dev):
        return pltpu.make_async_remote_copy(src_ref=src, dst_ref=dst, send_sem=ssem, recv_sem=rsem,
                                            device_id=dev, device_id_type=MESH)

    loads = [pltpu.make_async_copy(x_ref.at[pl.ds(c * ROWS, ROWS), pl.ds(j * TILE, TILE)], (zb.at[0, c, j] if c < NEAR else z2.at[0, j]),
                                   loc.at[c, j])
             for c in range(CHUNKS) for j in range(8)]
    for copy in loads:
        copy.start()
    om_load = pltpu.make_async_copy(om_ref.at[0], om.at[0, core], loc.at[CHUNKS, 0])
    om_load.start()

    partners = [zp, zm, cq, hp, hm] + [plane(dx, f) for dx in range(NX) for f in range(2) if dx or f]
    barrier = pltpu.get_barrier_semaphore()
    for dev in partners:
        pl.semaphore_signal(barrier, inc=1, device_id=dev, device_id_type=MESH)

    i0 = lax.broadcasted_iota(jnp.int32, (SLOTS, SLOTS), 0)
    i1 = lax.broadcasted_iota(jnp.int32, (SLOTS, SLOTS), 1)
    eye = i0 == i1
    rb = jnp.broadcast_to(rows_v[...], (SLOTS, SLOTS))
    cb = jnp.broadcast_to(cols_v[...], (SLOTS, SLOTS))
    rc = jnp.broadcast_to(jnp.sum(jnp.where(eye, rb, 0), axis=1, keepdims=True), (SLOTS, SLOTS))
    cc = jnp.sum(jnp.where(eye, cb, 0), axis=1, keepdims=True)
    rank = jnp.sum(jnp.where((rb < rc) | ((rb == rc) & (i1 < i0)), 1, 0), axis=1, keepdims=True)
    order = jnp.sum(jnp.where(rank == i1, i0, 0), axis=0, keepdims=True)
    last = jnp.sum(jnp.where(rc <= rb, 1, 0), axis=0, keepdims=True) - 1
    lane = lax.broadcasted_iota(jnp.int32, (SLOTS, 128), 1)
    ccw = jnp.broadcast_to(cc, (SLOTS, 128))
    wanted = jnp.sum(jnp.where((ccw >> 3) == lane, ccw & 7, 0), axis=0, keepdims=True)
    wq[0] = jnp.broadcast_to(wanted, (8, 128))
    tsm_v = wq.at[8]
    tsm_v[0:1, 0:SLOTS] = order
    tsm_v[1:2, 0:SLOTS] = last

    pl.semaphore_wait(barrier, len(partners))

    def w_copy(dx, f):
        place = dx * 2 + f
        return remote(wq.at[0], wq.at[place], wsend.at[place], wrecv.at[place], plane(dx, f))

    others = [(dx, f) for dx in range(NX) for f in range(2) if dx or f]
    for dx, f in others:
        w_copy(dx, f).start()
    t_copy = pltpu.make_async_copy(wq.at[8], tsm, loc.at[CHUNKS, 1])
    t_copy.start()

    def z_copy(d, k, c):
        if d == 0:
            return remote(zb.at[k - 1, c], zb.at[k, c], zs.at[0], zr.at[0, k, c], zp)
        return remote(zb.at[(9 - k) % 8, c], zb.at[8 - k, c], zs.at[1], zr.at[1, k, c], zm)

    def z_half(d, c):
        if d == 0:
            return remote(zb.at[3, c], zb.at[4, c], zsh.at[0], zr.at[0, 4, c], zp)
        return remote(zb.at[5, c], zb.at[4, c], zsh.at[1], zr.at[1, 4, c], zm)

    def z2_copy(d, k):
        if d == 0:
            return remote(z2.at[k - 1], z2.at[k], z2s.at[0], z2r.at[0, k], zp)
        return remote(z2.at[(9 - k) % 8], z2.at[8 - k], z2s.at[1], z2r.at[1, k], zm)

    z2_half = remote(z2.at[5], z2.at[4], z2h.at[0], z2r.at[1, 4], zm)
    gather_y = remote(z2.at[0, pl.ds(0, 8)], z2.at[0, pl.ds(8, 8)], gys.at[0], gyr.at[0], yq)

    def rows(c):
        return pl.ds(c * ROWS if isinstance(c, int) else pl.multiple_of(c * ROWS, ROWS), ROWS)

    def y_copy(k, c):
        return remote(ystg.at[k, c], rec.at[k, pl.ds(Y_XM, 4), rows(c)], ss.at[0], ys_r.at[k, c], yq)

    def send_own(k, c):
        for i, (place, dev) in enumerate(((XP_OWN, xp), (XM_OWN, xm), (X2_OWN, x2))):
            remote(stgx.at[k, c, i], rec.at[k, place, rows(c)], ss.at[1 + i], ends.at[i], dev).start()

    def send_pair(k, c):
        for i, (here, place, dev) in enumerate(((Y_XP, XP_PAIR, xp), (Y_XM, XM_PAIR, xm), (Y_X2, X2_PAIR, x2))):
            remote(rec.at[k, here, rows(c)], rec.at[k, place, rows(c)], ss.at[4 + i], ends.at[3 + i], dev).start()

    def choose(idx, panels):
        got = panels(0)
        for j in range(1, 8):
            got = jnp.where(idx == j, panels(j), got)
        return got

    def want(e, f, k, other):
        holder = ((z - k + NZ) % NZ) * 8 + x * 2 + (1 - y if other else y)
        return wsm[((NX - e) % NX) * 2 + f, 0, holder]

    def keep_own(k, c, e, got):
        if e == 0:
            rec[k, HERE, rows(c)] = got
        else:
            stgx[k, c, (0, 2, 1)[e - 1]] = got

    def pick(k, c):
        def panels(j):
            return zb[k, c, j]

        for e in range(NX):
            ystg[k, c, (3, 2, 1, 0)[e]] = choose(want(e, 1, k, False), panels)
        y_copy(k, c).start()
        for e in range(NX):
            keep_own(k, c, e, choose(want(e, 0, k, False), panels))
        send_own(k, c)

    def pick_whole(k):
        for e in range(NX):
            keep_own(k, NEAR, e, choose(want(e, 0, k, False), lambda j: z2[k, j]))
        send_own(k, NEAR)
        for e in range(NX):
            rec[k, (Y_ME, Y_XP, Y_X2, Y_XM)[e], rows(NEAR)] = choose(want(e, 0, k, True), lambda j: z2[k, 8 + j])
        send_pair(k, NEAR)

    def unit(u):
        v = u - NEAR
        far = v >= 6 * NEAR
        w = v - 6 * NEAR
        d = v // (2 * NEAR) + 1
        side = jnp.where(far, w % 2, v % 2)
        k = jnp.where(far, 4, jnp.where(side == 0, d, 8 - d))
        c = jnp.where(far, (2 * w) % 3, (v % (2 * NEAR)) // 2)
        first = u < NEAR
        return jnp.where(first, 0, k), jnp.where(first, u, c), d, side

    for j in range(8):
        loads[NEAR * 8 + j].wait()
    gather_y.start()
    for c in range(NEAR):
        for j in range(8):
            loads[c * 8 + j].wait()
        z_copy(0, 1, c).start()
        z_copy(1, 1, c).start()

    om_load.wait()

    def om_copy(d, what):
        far = hp if d == 0 else hm
        if what == 0:
            return remote(om.at[0, core], om.at[1 if d == 0 else 3, core], oms.at[d], omr.at[d], far)
        half = pl.ds(0 if d == 0 else 2, 2)
        return remote(om.at[1 if d == 0 else 3, core, half], om.at[2, core, half], oms.at[2 + d], omr.at[2 + d], far)

    def om_core(g):
        return remote(om.at[g, core], om.at[g, core], ocs.at[g], ocr.at[g], cq)

    om_copy(0, 0).start()
    om_copy(1, 0).start()
    om_core(0).start()

    for dx, f in others:
        w_copy(dx, f).wait_recv()
    w_load = pltpu.make_async_copy(wq.at[pl.ds(0, 8)], wsm, loc.at[CHUNKS, 2])
    w_load.start()
    w_load.wait()

    pick(0, 0)
    gather_y.wait_recv()
    z2_copy(0, 1).start()
    z2_copy(1, 1).start()
    for c in range(1, NEAR):
        pick(0, c)
    pick_whole(0)

    def y_step(u):
        k, c, _, _ = unit(u)
        y_copy(k, c).wait_recv()
        send_pair(k, c)

    def z_step(u):
        k, c, d, side = unit(u)

        @pl.when(side == 0)
        def _():
            z_copy(0, d, c).wait_recv()

            @pl.when(d < 3)
            def _():
                z_copy(0, d + 1, c).start()

            @pl.when((d == 3) & (c < 2))
            def _():
                z_half(0, c).start()

        @pl.when(side == 1)
        def _():
            z_copy(1, d, c).wait_recv()

            @pl.when(d < 3)
            def _():
                z_copy(1, d + 1, c).start()

            @pl.when((d == 3) & (c == 2))
            def _():
                z_half(1, c).start()

        pick(k, c)

    def whole_step(d):
        z2_copy(0, d).wait_recv()

        @pl.when(d < 3)
        def _():
            z2_copy(0, d + 1).start()

        z2_copy(1, d).wait_recv()

        @pl.when(d < 3)
        def _():
            z2_copy(1, d + 1).start()

        @pl.when(d == 3)
        def _():
            z2_half.start()

        pick_whole(d)
        pick_whole(8 - d)

    def step(u, carry):
        @pl.when(u < UNITS)
        def _():
            z_step(u)

        y_step(u - LAG)

        @pl.when((u < UNITS - 3) & (u % 6 == 2))
        def _():
            whole_step((u - NEAR) // 6 + 1)

        @pl.when(u == UNITS - 1)
        def _():
            z2_copy(1, 4).wait_recv()
            pick_whole(4)

        return carry

    lax.fori_loop(NEAR, OM_STEP, step, 0)
    om_copy(0, 0).wait_recv()
    om_copy(0, 1).start()
    om_core(1).start()
    om_copy(1, 0).wait_recv()
    om_copy(1, 1).start()
    om_core(3).start()
    lax.fori_loop(OM_STEP, UNITS + LAG, step, 0)
    om_copy(0, 1).wait_recv()
    om_copy(1, 1).wait_recv()
    om_core(2).start()
    t_copy.wait()
    for g in (0, 1, 3, 2):
        om_core(g).wait_recv()
    whole = rec.at[:, HERE]
    for i in range(6):
        pltpu.make_async_copy(whole, whole, ends.at[i]).wait()

    def panel(s):
        h = cols_s[0, s] >> 3
        k = (z - (h >> 3) + NZ) & (NZ - 1)
        dx = (x - ((h >> 1) & 3) + NX) & (NX - 1)
        other = (h & 1) != y
        own = jnp.where(dx == 0, HERE, jnp.where(dx == 1, XP_OWN, jnp.where(dx == 2, X2_OWN, XM_OWN)))
        pair = jnp.where(dx == 0, Y_ME, jnp.where(dx == 1, XP_PAIR, jnp.where(dx == 2, X2_PAIR, XM_PAIR)))
        return rec[k, jnp.where(other, pair, own)]

    def row_step(i, before):
        s = tsm[0, i]
        row = rows_s[0, s]
        who = s >> 2
        tile = om[(yh - (who >> 1) + NH) & (NH - 1), who & 1, s & 3]
        prod = lax.dot_general(tile, panel(s), (((1,), (1,)), ((), ())), preferred_element_type=jnp.float32)
        total = jnp.where(row == before, acc[...], 0.0) + prod
        acc[...] = total
        yb[i] = total.astype(jnp.bfloat16)
        return row

    acc[...] = jnp.zeros_like(acc)
    lax.fori_loop(0, SLOTS, row_step, jnp.int32(-1))

    def grad(g, who, i):
        s = (((yh + g) % NH) * 2 + who) * 4 + i
        return jnp.dot(yb[tsm[1, s]], panel(s), preferred_element_type=jnp.float32)

    def for_pair(g):
        def one(i, carry):
            gx[g, i] = grad(g, 1 - core, i).astype(jnp.bfloat16)
            return carry

        lax.fori_loop(0, 4, one, 0)
        pair_copy(g).start()

    def for_me(g):
        def one(i, carry):
            gown[g, i] = grad(g, core, i)
            return carry

        lax.fori_loop(0, 4, one, 0)

    def pair_copy(g):
        return remote(gx.at[g], grx.at[g], gs.at[g], gr.at[g], cq)

    def half_copy(d):
        half = pl.ds(2 * d, 2)
        return remote(hs.at[half], relr.at[half], hss.at[d], hsr.at[d], hp if d == 0 else hm)

    def last_copy(d, h):
        half = pl.ds(2 * h, 2)
        return remote(fs.at[d, half], fr.at[d, half], fss.at[d, h], fsr.at[d, h], hp if d == 0 else hm)

    for_pair(2)
    for_pair(1)
    for_pair(3)
    for_me(2)
    pair_copy(2).wait_recv()
    hs[...] = (gown[2] + grx[2].astype(jnp.float32)).astype(jnp.bfloat16)
    half_copy(0).start()
    half_copy(1).start()
    for_me(1)
    for_me(3)
    for d, g in ((0, 1), (1, 3)):
        direct = 1 - d
        half = slice(2 * direct, 2 * direct + 2)
        pair_copy(g).wait_recv()
        fs[d, half] = (gown[g, half] + grx[g, half].astype(jnp.float32)).astype(jnp.bfloat16)
        last_copy(d, direct).start()
    for_pair(0)
    for_me(0)
    for d, g in ((0, 1), (1, 3)):
        half = slice(2 * d, 2 * d + 2)
        half_copy(d).wait_recv()
        fs[d, half] = (gown[g, half] + grx[g, half].astype(jnp.float32)
                       + relr[half].astype(jnp.float32)).astype(jnp.bfloat16)
        last_copy(d, d).start()
    pair_copy(0).wait_recv()
    for d in range(2):
        for h in range(2):
            last_copy(d, h).wait_recv()

    e0 = lax.broadcasted_iota(jnp.int32, (TILE, TILE), 0)
    e1 = lax.broadcasted_iota(jnp.int32, (TILE, TILE), 1)
    for i in range(4):
        s = t * 4 + i
        total = (gown[0, i] + grx[0, i].astype(jnp.float32)) + (fr[0, i].astype(jnp.float32) + fr[1, i].astype(jnp.float32))
        own = om[0, core, i].astype(jnp.float32)
        diag = jnp.where(rows_s[0, s] == cols_s[0, s], e0, -1) == e1
        inverse = jnp.where(diag, 1.0 / jnp.where(diag, own, 1.0), 0.0)
        stepped = own - 0.5 * (total / 2048.0 - inverse)
        shrunk = stepped - jnp.clip(stepped, -0.05, 0.05)
        out_ref[0, i] = jnp.where(diag, stepped, shrunk).astype(jnp.bfloat16)

    for dx, f in others:
        w_copy(dx, f).wait_send()
    gather_y.wait_send()
    z2_half.wait_send()
    for d in range(2):
        three, three2 = zb.at[pl.ds(0, 3)], z2.at[pl.ds(0, 3)]
        pltpu.make_async_copy(three, three, zs.at[d]).wait()
        pltpu.make_async_copy(three2, three2, z2s.at[d]).wait()
        rest = zb.at[3, pl.ds(0, 2 - d)]
        pltpu.make_async_copy(rest, rest, zsh.at[d]).wait()
        om_copy(d, 0).wait_send()
        om_copy(d, 1).wait_send()
        half_copy(d).wait_send()
        for h in range(2):
            last_copy(d, h).wait_send()
    for g in range(4):
        om_core(g).wait_send()
        pair_copy(g).wait_send()
    pltpu.make_async_copy(ystg, ystg, ss.at[0]).wait()
    for i in range(6):
        pltpu.make_async_copy(whole, whole, ss.at[1 + i]).wait()


def body(xdata, omega_tiles, tile_rows, tile_cols):
    bf, f32, i32 = jnp.bfloat16, jnp.float32, jnp.int32
    tile = (TILE, TILE)
    dma = pltpu.SemaphoreType.DMA
    vmem = pl.BlockSpec(memory_space=pltpu.VMEM)
    smem = pl.BlockSpec(memory_space=pltpu.SMEM)
    hbm = pl.BlockSpec(memory_space=pl.ANY)
    return pl.pallas_call(
        kernel,
        out_shape=jax.ShapeDtypeStruct(omega_tiles.shape, bf),
        in_specs=[hbm, hbm, vmem, vmem, smem, smem],
        out_specs=vmem,
        scratch_shapes=[
            pltpu.VMEM((NZ, NEAR, 8, ROWS, TILE), bf),
            pltpu.VMEM((NZ, 16, ROWS, TILE), bf),
            pltpu.VMEM((NZ, CHUNKS, 3, ROWS, TILE), bf),
            pltpu.VMEM((NZ, NEAR, 4, ROWS, TILE), bf),
            pltpu.VMEM((NZ, 11) + tile, bf),
            pltpu.VMEM((NH, 2, 4) + tile, bf),
            pltpu.VMEM((SLOTS,) + tile, bf),
            pltpu.VMEM(tile, f32),
            pltpu.VMEM((NH, 4) + tile, bf),
            pltpu.VMEM((NH, 4) + tile, bf),
            pltpu.VMEM((NH, 4) + tile, f32),
            pltpu.VMEM((4,) + tile, bf),
            pltpu.VMEM((4,) + tile, bf),
            pltpu.VMEM((2, 4) + tile, bf),
            pltpu.VMEM((2, 4) + tile, bf),
            pltpu.VMEM((9, 8, 128), i32),
            pltpu.SMEM((8, 8, 128), i32),
            pltpu.SMEM((8, 128), i32),
            dma((2,)), dma((2,)), dma((2, 5, NEAR)),
            dma((2,)), dma((1,)), dma((2, 5)), dma((1,)), dma((1,)),
            dma((7,)), dma((NZ, NEAR)), dma((6,)),
            dma((8,)), dma((8,)),
            dma((4,)), dma((4,)), dma((4,)), dma((4,)),
            dma((4,)), dma((4,)), dma((2,)), dma((2,)), dma((2, 2)), dma((2, 2)),
            dma((CHUNKS + 1, 8)),
        ],
        compiler_params=pltpu.CompilerParams(
            collective_id=0, has_side_effects=True, vmem_limit_bytes=60 * 1024 * 1024
        ),
    )(xdata, omega_tiles, tile_rows, tile_cols, tile_rows, tile_cols)


def solution(mesh):
    return jax.shard_map(
        body,
        mesh=mesh,
        in_specs=(P("team", "blk"), P("blk", "team", None, None), P("blk", None), P("blk", None)),
        out_specs=P("blk", "team", None, None),
        check_vma=False,
    )
```

```python
import jax
import jax.numpy as jnp
from jax import lax
from jax.experimental import pallas as pl
from jax.experimental.pallas import tpu as pltpu
from jax.sharding import PartitionSpec as P

MESH = pl.DeviceIdType.MESH
NZ, NX, NH = 8, 4, 4
TILE = 256
SLOTS = 32
PARTS = (64, 64, 48)
STARTS = (0, 64, 128)
PAIR_START, PAIR_ROWS = 176, 80
OWN, OTHER = 3, 4
OM_STEP = 2


def kernel(x_ref, om_ref, rows_v, cols_v, rows_s, cols_s, out_ref,
           zb0, zb1, zb2, z2, st0, st1, st2, stp, rec, om, yb, acc, gx, grx, gown, hs, relr, fs, fr, wq, wsm, tsm,
           zs, zsh, zr, gys, gyr, near_s, near_r, pair_s, pair_r,
           wsend, wrecv, oms, omr, ocs, ocr, gs, gr, hss, hsr, fss, fsr, loc):
    zb, st = (zb0, zb1, zb2), (st0, st1, st2)
    t = lax.axis_index("team")
    b = lax.axis_index("blk")
    core, yh = t % 2, t // 2
    z, x, y = b // 8, (b // 2) % 4, b % 2

    def plane(dx, f):
        yy = 1 - y if f else y
        return (t, z * 8 + ((x + dx) % NX) * 2 + yy)

    zp = (t, ((z + 1) % NZ) * 8 + b % 8)
    zm = (t, ((z + NZ - 1) % NZ) * 8 + b % 8)
    yq = plane(0, 1)
    cq = (yh * 2 + 1 - core, b)
    hp = (((yh + 1) % NH) * 2 + core, b)
    hm = (((yh + 3) % NH) * 2 + core, b)

    def remote(src, dst, ssem, rsem, dev):
        return pltpu.make_async_remote_copy(src_ref=src, dst_ref=dst, send_sem=ssem, recv_sem=rsem,
                                            device_id=dev, device_id_type=MESH)

    x_loads = []
    for c, (start, size) in enumerate(zip(STARTS + (PAIR_START,), PARTS + (PAIR_ROWS,))):
        x_loads.append([pltpu.make_async_copy(x_ref.at[pl.ds(start, size), pl.ds(j * TILE, TILE)],
                                              (zb[c] if c < OWN else z2).at[0, j], loc.at[c, j]) for j in range(8)])
    for c in (OWN, 0, 1, 2):
        for copy in x_loads[c]:
            copy.start()
    om_load = pltpu.make_async_copy(om_ref.at[0], om.at[0, core], loc.at[4, 0])
    om_load.start()

    partners = [zp, zm, cq, hp, hm] + [plane(dx, f) for dx in range(NX) for f in range(2) if dx or f]
    barrier = pltpu.get_barrier_semaphore()
    for dev in partners:
        pl.semaphore_signal(barrier, inc=1, device_id=dev, device_id_type=MESH)

    i0 = lax.broadcasted_iota(jnp.int32, (SLOTS, SLOTS), 0)
    i1 = lax.broadcasted_iota(jnp.int32, (SLOTS, SLOTS), 1)
    eye = i0 == i1
    rb = jnp.broadcast_to(rows_v[...], (SLOTS, SLOTS))
    cb = jnp.broadcast_to(cols_v[...], (SLOTS, SLOTS))
    rc = jnp.broadcast_to(jnp.sum(jnp.where(eye, rb, 0), axis=1, keepdims=True), (SLOTS, SLOTS))
    cc = jnp.sum(jnp.where(eye, cb, 0), axis=1, keepdims=True)
    rank = jnp.sum(jnp.where((rb < rc) | ((rb == rc) & (i1 < i0)), 1, 0), axis=1, keepdims=True)
    order = jnp.sum(jnp.where(rank == i1, i0, 0), axis=0, keepdims=True)
    last = jnp.sum(jnp.where(rc <= rb, 1, 0), axis=0, keepdims=True) - 1
    lane = lax.broadcasted_iota(jnp.int32, (SLOTS, 128), 1)
    ccw = jnp.broadcast_to(cc, (SLOTS, 128))
    wanted = jnp.sum(jnp.where((ccw >> 3) == lane, ccw & 7, 0), axis=0, keepdims=True)
    wq[0] = jnp.broadcast_to(wanted, (8, 128))
    tsm_v = wq.at[8]
    tsm_v[0:1, 0:SLOTS] = order
    tsm_v[1:2, 0:SLOTS] = last

    pl.semaphore_wait(barrier, len(partners))

    def w_copy(dx, f):
        place = dx * 2 + f
        return remote(wq.at[0], wq.at[place], wsend.at[place], wrecv.at[place], plane(dx, f))

    others = [(dx, f) for dx in range(NX) for f in range(2) if dx or f]
    for dx, f in others:
        w_copy(dx, f).start()
    t_copy = pltpu.make_async_copy(wq.at[8], tsm, loc.at[4, 1])
    t_copy.start()

    def z_ref(u, k):
        if u < OWN:
            return zb[u].at[k]
        return z2.at[k, pl.ds(0 if u == OWN else 8, 8)]

    def z_copy(d, k, u, last=False):
        send = zsh.at[u] if last else zs.at[d, u]
        if d == 0:
            return remote(z_ref(u, k - 1), z_ref(u, k), send, zr.at[0, k, u], zp)
        return remote(z_ref(u, (9 - k) % 8), z_ref(u, 8 - k), send, zr.at[1, k, u], zm)

    def way_of_last(u):
        return 0 if u < OWN else 1

    gather_y = remote(z2.at[0, pl.ds(0, 8)], z2.at[0, pl.ds(8, 8)], gys.at[0], gyr.at[0], yq)

    def choose(e, f, k, other, panels):
        holder = ((z - k + NZ) % NZ) * 8 + x * 2 + (1 - y if other else y)
        idx = wsm[((NX - e) % NX) * 2 + f, 0, holder]
        got = panels(0)
        for j in range(1, 8):
            got = jnp.where(idx == j, panels(j), got)
        return got

    def near_rows(u):
        return pl.ds(STARTS[u], PARTS[u])

    pair_rows = pl.ds(PAIR_START, PAIR_ROWS)

    def near_copy(u, k, i):
        e, f = others[i]
        return remote(st[u].at[k, i], rec.at[k, e, f, near_rows(u)], near_s.at[u, i], near_r.at[u, i], plane(e, f))

    def pair_copies(k, e, half):
        return remote(stp.at[k, half, e - 1], rec.at[k, e, half, pair_rows], pair_s.at[half, e], pair_r.at[half, e], plane(e, 0))

    def pick(u, k):
        if u < OWN:
            for i in (0, 2, 4, 6, 1, 3, 5):
                e, f = others[i]
                st[u][k, i] = choose(e, f, k, False, lambda j: zb[u][k, j])
                near_copy(u, k, i).start()
            rec[k, 0, 0, near_rows(u)] = choose(0, 0, k, False, lambda j: zb[u][k, j])
            return
        half = u - OWN
        for e in (2, 1, 3, 0):
            got = choose(e, 0, k, half == 1, lambda j: z2[k, 8 * half + j])
            if e == 0:
                rec[k, 0, half, pair_rows] = got
            else:
                stp[k, half, e - 1] = got
                pair_copies(k, e, half).start()

    for u in (OWN, 0, 1, 2):
        for copy in x_loads[u]:
            copy.wait()
        if u == OWN:
            gather_y.start()
        z_copy(0, 1, u).start()
        z_copy(1, 1, u).start()

    om_load.wait()

    def om_copy(d, what):
        far = hp if d == 0 else hm
        if what == 0:
            return remote(om.at[0, core], om.at[1 if d == 0 else 3, core], oms.at[d], omr.at[d], far)
        half = pl.ds(0 if d == 0 else 2, 2)
        return remote(om.at[1 if d == 0 else 3, core, half], om.at[2, core, half], oms.at[2 + d], omr.at[2 + d], far)

    def om_core(g):
        return remote(om.at[g, core], om.at[g, core], ocs.at[g], ocr.at[g], cq)

    om_copy(0, 0).start()
    om_copy(1, 0).start()
    om_core(0).start()

    for dx, f in others:
        w_copy(dx, f).wait_recv()
    w_load = pltpu.make_async_copy(wq.at[pl.ds(0, 8)], wsm, loc.at[4, 2])
    w_load.start()
    w_load.wait()

    for u in (OWN, 0, 1, 2):
        pick(u, 0)
    gather_y.wait_recv()
    z_copy(0, 1, OTHER).start()
    z_copy(1, 1, OTHER).start()
    pick(OTHER, 0)

    def step(d, carry):
        for u in (OWN, 0, 1, 2, OTHER):
            for way in range(2):
                z_copy(way, d, u).wait_recv()

                @pl.when(d < 3)
                def _():
                    z_copy(way, d + 1, u).start()

                if way == way_of_last(u):
                    @pl.when(d == 3)
                    def _():
                        z_copy(way, 4, u, True).start()

            pick(u, d)
            pick(u, 8 - d)
        return carry

    lax.fori_loop(1, OM_STEP, step, 0)
    om_copy(0, 0).wait_recv()
    om_copy(0, 1).start()
    om_core(1).start()
    om_copy(1, 0).wait_recv()
    om_copy(1, 1).start()
    om_core(3).start()
    lax.fori_loop(OM_STEP, 4, step, 0)
    for u in (0, OWN, 1, OTHER, 2):
        z_copy(way_of_last(u), 4, u, True).wait_recv()
        pick(u, 4)
    om_copy(0, 1).wait_recv()
    om_copy(1, 1).wait_recv()
    om_core(2).start()
    t_copy.wait()
    for g in (0, 1, 3, 2):
        om_core(g).wait_recv()

    def wait_all(ref, sem):
        pltpu.make_async_copy(ref, ref, sem).wait()

    for u in range(3):
        for i in range(7):
            wait_all(st[u].at[:, 0], near_r.at[u, i])
    for half in range(2):
        for e in range(1, NX):
            wait_all(stp.at[:, 0, 0], pair_r.at[half, e])

    def panel(s):
        h = cols_s[0, s] >> 3
        return rec[(z - (h >> 3) + NZ) & (NZ - 1), (x - ((h >> 1) & 3) + NX) & (NX - 1), (h & 1) ^ y]

    def row_step(i, before):
        s = tsm[0, i]
        row = rows_s[0, s]
        who = s >> 2
        tile = om[(yh - (who >> 1) + NH) & (NH - 1), who & 1, s & 3]
        prod = lax.dot_general(tile, panel(s), (((1,), (1,)), ((), ())), preferred_element_type=jnp.float32)
        total = jnp.where(row == before, acc[...], 0.0) + prod
        acc[...] = total
        yb[i] = total.astype(jnp.bfloat16)
        return row

    acc[...] = jnp.zeros_like(acc)
    lax.fori_loop(0, SLOTS, row_step, jnp.int32(-1), unroll=4)

    def grad(g, who, i):
        s = (((yh + g) % NH) * 2 + who) * 4 + i
        return jnp.dot(yb[tsm[1, s]], panel(s), preferred_element_type=jnp.float32)

    def for_pair(g):
        def one(i, carry):
            gx[g, i] = grad(g, 1 - core, i).astype(jnp.bfloat16)
            return carry

        lax.fori_loop(0, 4, one, 0, unroll=4)
        pair_copy(g).start()

    def for_me(g):
        def one(i, carry):
            gown[g, i] = grad(g, core, i)
            return carry

        lax.fori_loop(0, 4, one, 0, unroll=4)

    def pair_copy(g):
        return remote(gx.at[g], grx.at[g], gs.at[g], gr.at[g], cq)

    def half_copy(d):
        half = pl.ds(2 * d, 2)
        return remote(hs.at[half], relr.at[half], hss.at[d], hsr.at[d], hp if d == 0 else hm)

    def last_copy(d, h):
        half = pl.ds(2 * h, 2)
        return remote(fs.at[d, half], fr.at[d, half], fss.at[d, h], fsr.at[d, h], hp if d == 0 else hm)

    for_pair(2)
    for_pair(1)
    for_pair(3)
    for_me(2)
    pair_copy(2).wait_recv()
    hs[...] = (gown[2] + grx[2].astype(jnp.float32)).astype(jnp.bfloat16)
    half_copy(0).start()
    half_copy(1).start()
    for_me(1)
    for_me(3)
    for d, g in ((0, 1), (1, 3)):
        direct = 1 - d
        half = slice(2 * direct, 2 * direct + 2)
        pair_copy(g).wait_recv()
        fs[d, half] = (gown[g, half] + grx[g, half].astype(jnp.float32)).astype(jnp.bfloat16)
        last_copy(d, direct).start()
    for_pair(0)
    for_me(0)
    for d, g in ((0, 1), (1, 3)):
        half = slice(2 * d, 2 * d + 2)
        half_copy(d).wait_recv()
        fs[d, half] = (gown[g, half] + grx[g, half].astype(jnp.float32)
                       + relr[half].astype(jnp.float32)).astype(jnp.bfloat16)
        last_copy(d, d).start()
    pair_copy(0).wait_recv()
    for d in range(2):
        for h in range(2):
            last_copy(d, h).wait_recv()

    e0 = lax.broadcasted_iota(jnp.int32, (TILE, TILE), 0)
    e1 = lax.broadcasted_iota(jnp.int32, (TILE, TILE), 1)
    for i in range(4):
        s = t * 4 + i
        total = (gown[0, i] + grx[0, i].astype(jnp.float32)) + (fr[0, i].astype(jnp.float32) + fr[1, i].astype(jnp.float32))
        own = om[0, core, i].astype(jnp.float32)
        diag = jnp.where(rows_s[0, s] == cols_s[0, s], e0, -1) == e1
        inverse = jnp.where(diag, 1.0 / jnp.where(diag, own, 1.0), 0.0)
        stepped = own - 0.5 * (total / 2048.0 - inverse)
        shrunk = stepped - jnp.clip(stepped, -0.05, 0.05)
        out_ref[0, i] = jnp.where(diag, stepped, shrunk).astype(jnp.bfloat16)

    for dx, f in others:
        w_copy(dx, f).wait_send()
    gather_y.wait_send()
    for u in range(5):
        z_copy(way_of_last(u), 4, u, True).wait_send()
        for d in range(2):
            wait_all((zb[u] if u < OWN else z2).at[pl.ds(0, 3), pl.ds(0, 8)], zs.at[d, u])
    for d in range(2):
        om_copy(d, 0).wait_send()
        om_copy(d, 1).wait_send()
        half_copy(d).wait_send()
        for h in range(2):
            last_copy(d, h).wait_send()
    for g in range(4):
        om_core(g).wait_send()
        pair_copy(g).wait_send()
    for u in range(3):
        for i in range(7):
            wait_all(st[u].at[:, 0], near_s.at[u, i])
    for half in range(2):
        for e in range(1, NX):
            wait_all(stp.at[:, 0, 0], pair_s.at[half, e])


def body(xdata, omega_tiles, tile_rows, tile_cols):
    bf, f32, i32 = jnp.bfloat16, jnp.float32, jnp.int32
    tile = (TILE, TILE)
    dma = pltpu.SemaphoreType.DMA
    vmem = pl.BlockSpec(memory_space=pltpu.VMEM)
    smem = pl.BlockSpec(memory_space=pltpu.SMEM)
    hbm = pl.BlockSpec(memory_space=pl.ANY)
    return pl.pallas_call(
        kernel,
        out_shape=jax.ShapeDtypeStruct(omega_tiles.shape, bf),
        in_specs=[hbm, hbm, vmem, vmem, smem, smem],
        out_specs=vmem,
        scratch_shapes=[
            *[pltpu.VMEM((NZ, 8, size, TILE), bf) for size in PARTS],
            pltpu.VMEM((NZ, 16, PAIR_ROWS, TILE), bf),
            *[pltpu.VMEM((NZ, 7, size, TILE), bf) for size in PARTS],
            pltpu.VMEM((NZ, 2, 3, PAIR_ROWS, TILE), bf),
            pltpu.VMEM((NZ, NX, 2) + tile, bf),
            pltpu.VMEM((NH, 2, 4) + tile, bf),
            pltpu.VMEM((SLOTS,) + tile, bf),
            pltpu.VMEM(tile, f32),
            pltpu.VMEM((NH, 4) + tile, bf),
            pltpu.VMEM((NH, 4) + tile, bf),
            pltpu.VMEM((NH, 4) + tile, f32),
            pltpu.VMEM((4,) + tile, bf),
            pltpu.VMEM((4,) + tile, bf),
            pltpu.VMEM((2, 4) + tile, bf),
            pltpu.VMEM((2, 4) + tile, bf),
            pltpu.VMEM((9, 8, 128), i32),
            pltpu.SMEM((8, 8, 128), i32),
            pltpu.SMEM((8, 128), i32),
            dma((2, 5)), dma((5,)), dma((2, 5, 5)),
            dma((1,)), dma((1,)),
            dma((3, 7)), dma((3, 7)), dma((2, 4)), dma((2, 4)),
            dma((8,)), dma((8,)),
            dma((4,)), dma((4,)), dma((4,)), dma((4,)),
            dma((4,)), dma((4,)), dma((2,)), dma((2,)), dma((2, 2)), dma((2, 2)),
            dma((5, 8)),
        ],
        compiler_params=pltpu.CompilerParams(
            collective_id=0, has_side_effects=True, vmem_limit_bytes=60 * 1024 * 1024
        ),
    )(xdata, omega_tiles, tile_rows, tile_cols, tile_rows, tile_cols)


def solution(mesh):
    return jax.shard_map(
        body,
        mesh=mesh,
        in_specs=(P("team", "blk"), P("blk", "team", None, None), P("blk", None), P("blk", None)),
        out_specs=P("blk", "team", None, None),
        check_vma=False,
    )
```

```python
import jax
import jax.numpy as jnp
from jax import lax
from jax.experimental import pallas as pl
from jax.experimental.pallas import tpu as pltpu
from jax.sharding import PartitionSpec as P

MESH = pl.DeviceIdType.MESH
NZ, NX, NH = 8, 4, 4
TILE = 256
SLOTS = 32
PARTS = (64, 64, 48)
STARTS = (0, 64, 128)
PAIR_START, PAIR_ROWS = 176, 80
OWN, OTHER = 3, 4


def kernel(x_ref, om_ref, rows_v, cols_v, rows_s, cols_s, out_ref,
           zb0, zb1, zb2, z2, st0, st1, st2, stp, sn0, sn1, sn2, snp, rec, om, yb, acc, gx, grx, gown, hs, relr, fs, fr, wq, wqn, wsm, wsn, tsm,
           zs0, zs, zr, gys, gyr, near_s, near_r, pair_s, pair_r,
           next_s, next_r, wsend, wrecv, wns, wnr, oms, omr, ocs, ocr, gs, gr, hss, hsr, fss, fsr, loc):
    zb, st, sn = (zb0, zb1, zb2), (st0, st1, st2), (sn0, sn1, sn2)
    t = lax.axis_index("team")
    b = lax.axis_index("blk")
    core, yh = t % 2, t // 2
    z, x, y = b // 8, (b // 2) % 4, b % 2

    def plane(dx, f, dz=0):
        yy = 1 - y if f else y
        return (t, ((z + dz) % NZ) * 8 + ((x + dx) % NX) * 2 + yy)

    zp, zm = plane(0, 0, 1), plane(0, 0, NZ - 1)
    yq = plane(0, 1)
    cq = (yh * 2 + 1 - core, b)
    hp = (((yh + 1) % NH) * 2 + core, b)
    hm = (((yh + 3) % NH) * 2 + core, b)

    def remote(src, dst, ssem, rsem, dev):
        return pltpu.make_async_remote_copy(src_ref=src, dst_ref=dst, send_sem=ssem, recv_sem=rsem,
                                            device_id=dev, device_id_type=MESH)

    x_loads = []
    for c, (start, size) in enumerate(zip(STARTS + (PAIR_START,), PARTS + (PAIR_ROWS,))):
        x_loads.append([pltpu.make_async_copy(x_ref.at[pl.ds(start, size), pl.ds(j * TILE, TILE)],
                                              (zb[c] if c < OWN else z2).at[0, j], loc.at[c, j]) for j in range(8)])
    for c in (OWN, 0, 1, 2):
        for copy in x_loads[c]:
            copy.start()
    om_load = pltpu.make_async_copy(om_ref.at[0], om.at[0, core], loc.at[4, 0])
    om_load.start()

    partners = [zp, zm, cq, hp, hm] + [plane(dx, f) for dx in range(NX) for f in range(2) if dx or f]
    barrier = pltpu.get_barrier_semaphore()
    for dev in partners:
        pl.semaphore_signal(barrier, inc=1, device_id=dev, device_id_type=MESH)

    i0 = lax.broadcasted_iota(jnp.int32, (SLOTS, SLOTS), 0)
    i1 = lax.broadcasted_iota(jnp.int32, (SLOTS, SLOTS), 1)
    eye = i0 == i1
    rb = jnp.broadcast_to(rows_v[...], (SLOTS, SLOTS))
    cb = jnp.broadcast_to(cols_v[...], (SLOTS, SLOTS))
    rc = jnp.broadcast_to(jnp.sum(jnp.where(eye, rb, 0), axis=1, keepdims=True), (SLOTS, SLOTS))
    cc = jnp.sum(jnp.where(eye, cb, 0), axis=1, keepdims=True)
    rank = jnp.sum(jnp.where((rb < rc) | ((rb == rc) & (i1 < i0)), 1, 0), axis=1, keepdims=True)
    order = jnp.sum(jnp.where(rank == i1, i0, 0), axis=0, keepdims=True)
    last = jnp.sum(jnp.where(rc <= rb, 1, 0), axis=0, keepdims=True) - 1
    lane = lax.broadcasted_iota(jnp.int32, (SLOTS, 128), 1)
    ccw = jnp.broadcast_to(cc, (SLOTS, 128))
    wanted = jnp.sum(jnp.where((ccw >> 3) == lane, ccw & 7, 0), axis=0, keepdims=True)
    wq[0] = jnp.broadcast_to(wanted, (8, 128))
    tsm_v = wq.at[8]
    tsm_v[0:1, 0:SLOTS] = order
    tsm_v[1:2, 0:SLOTS] = last

    pl.semaphore_wait(barrier, len(partners))

    def w_copy(dx, f):
        place = dx * 2 + f
        return remote(wq.at[0], wq.at[place], wsend.at[place], wrecv.at[place], plane(dx, f))

    others = [(dx, f) for dx in range(NX) for f in range(2) if dx or f]
    for dx, f in others:
        w_copy(dx, f).start()
    t_copy = pltpu.make_async_copy(wq.at[8], tsm, loc.at[4, 1])
    t_copy.start()

    def z_ref(u, k):
        if u < OWN:
            return zb[u].at[k]
        return z2.at[k, pl.ds(0 if u == OWN else 8, 8)]

    def z_copy(d, k, u):
        send = (zs0 if k == 1 else zs).at[d, u]
        if d == 0:
            return remote(z_ref(u, k - 1), z_ref(u, k), send, zr.at[0, k, u], zp)
        return remote(z_ref(u, (9 - k) % 8), z_ref(u, 8 - k), send, zr.at[1, k, u], zm)

    gather_y = remote(z2.at[0, pl.ds(0, 8)], z2.at[0, pl.ds(8, 8)], gys.at[0], gyr.at[0], yq)

    def choose(e, f, k, other, panels, way=None):
        holder = ((z - k + NZ) % NZ) * 8 + x * 2 + (1 - y if other else y)
        place = ((NX - e) % NX) * 2 + f
        idx = wsm[place, 0, holder] if way is None else wsn[way, place, 0, holder]
        got = panels(0)
        for j in range(1, 8):
            got = jnp.where(idx == j, panels(j), got)
        return got

    def near_rows(u):
        return pl.ds(STARTS[u], PARTS[u])

    pair_rows = pl.ds(PAIR_START, PAIR_ROWS)

    def near_copy(u, k, i):
        e, f = others[i]
        return remote(st[u].at[k, i], rec.at[k, e, f, near_rows(u)], near_s.at[u, i], near_r.at[u, i], plane(e, f))

    def pair_copies(k, e, half):
        return remote(stp.at[k, half, e - 1], rec.at[k, e, half, pair_rows], pair_s.at[half, e], pair_r.at[half, e], plane(e, 0))

    def pick(u, k):
        if u < OWN:
            for i in (0, 2, 4, 6, 1, 3, 5):
                e, f = others[i]
                st[u][k, i] = choose(e, f, k, False, lambda j: zb[u][k, j])
                near_copy(u, k, i).start()
            rec[k, 0, 0, near_rows(u)] = choose(0, 0, k, False, lambda j: zb[u][k, j])
            return
        half = u - OWN
        for e in (2, 1, 3, 0):
            got = choose(e, 0, k, half == 1, lambda j: z2[k, 8 * half + j])
            if e == 0:
                rec[k, 0, half, pair_rows] = got
            else:
                stp[k, half, e - 1] = got
                pair_copies(k, e, half).start()

    def next_copy(u, k, way, e, f):
        dev = plane(e, f if u < OWN else 0, 1 if way == 0 else NZ - 1)
        there = rec.at[k + 1 if way == 0 else k - 1, e, f, near_rows(u) if u < OWN else pair_rows]
        here = sn[u].at[way, e * 2 + f] if u < OWN else snp.at[way, f, e]
        return remote(here, there, next_s.at[way, u], next_r.at[way, u], dev)

    def pick_next(u, k, way):
        for e in (2, 1, 3, 0):
            if u < OWN:
                for f in (1, 0):
                    sn[u][way, e * 2 + f] = choose(e, f, k, False, lambda j: zb[u][k, j], way)
                    next_copy(u, k, way, e, f).start()
            else:
                half = u - OWN
                snp[way, half, e] = choose(e, 0, k, half == 1, lambda j: z2[k, 8 * half + j], way)
                next_copy(u, k, way, e, half).start()

    def first_z(u):
        for way in range(2):
            z_copy(way, 1, u).start()

    for u in (OWN, 0, 1, 2):
        for copy in x_loads[u]:
            copy.wait()
        if u == OWN:
            gather_y.start()
        if u != 2:
            first_z(u)

    om_load.wait()

    def om_copy(d, what):
        far = hp if d == 0 else hm
        if what == 0:
            return remote(om.at[0, core], om.at[1 if d == 0 else 3, core], oms.at[d], omr.at[d], far)
        half = pl.ds(0 if d == 0 else 2, 2)
        return remote(om.at[1 if d == 0 else 3, core, half], om.at[2, core, half], oms.at[2 + d], omr.at[2 + d], far)

    def om_core(g):
        return remote(om.at[g, core], om.at[g, core], ocs.at[g], ocr.at[g], cq)


    for dx, f in others:
        w_copy(dx, f).wait_recv()
    w_load = pltpu.make_async_copy(wq.at[pl.ds(0, 8)], wsm, loc.at[4, 2])
    w_load.start()
    table_up = remote(wq.at[pl.ds(0, 8)], wqn.at[1], wns.at[0], wnr.at[1], zp)
    table_down = remote(wq.at[pl.ds(0, 8)], wqn.at[0], wns.at[1], wnr.at[0], zm)
    table_up.start()
    table_down.start()
    w_load.wait()

    pick(OWN, 0)
    for way in range(2):
        z_copy(way, 1, OWN).wait_send()
    first_z(2)
    pick(0, 0)
    gather_y.wait_recv()
    for way in range(2):
        z_copy(way, 1, 0).wait_send()
    first_z(OTHER)
    for u in (1, 2, OTHER):
        pick(u, 0)

    for u in (OWN, 0, 1, 2, OTHER):
        for way in range(2):
            z_copy(way, 1, u).wait_recv()
            z_copy(way, 2, u).start()
        pick(u, 1)
        pick(u, 7)
        if u == 0:
            om_copy(0, 0).start()
            om_copy(1, 0).start()
            om_core(0).start()

    table_up.wait_recv()
    table_down.wait_recv()
    n_load = pltpu.make_async_copy(wqn, wsn, loc.at[4, 3])
    n_load.start()
    n_load.wait()

    for u in (OWN, 0, 1, 2, OTHER):
        short = 1 if u < OWN else 0
        for way in range(2):
            z_copy(way, 2, u).wait_recv()
            if way != short:
                z_copy(way, 3, u).start()
            else:
                pick_next(u, 2 if way == 0 else 6, way)
        pick(u, 2)
        pick(u, 6)
        if u == 1:
            om_copy(0, 0).wait_recv()
            om_copy(0, 1).start()
            om_core(1).start()
            om_copy(1, 0).wait_recv()
            om_copy(1, 1).start()
            om_core(3).start()

    for u in (OWN, 0, 1, 2, OTHER):
        way = 0 if u < OWN else 1
        z_copy(way, 3, u).wait_recv()
        pick_next(u, 3 if way == 0 else 5, way)
        pick(u, 3 if way == 0 else 5)

    om_copy(0, 1).wait_recv()
    om_copy(1, 1).wait_recv()
    om_core(2).start()
    t_copy.wait()
    for g in (0, 1, 3, 2):
        om_core(g).wait_recv()

    def wait_all(ref, sem):
        pltpu.make_async_copy(ref, ref, sem).wait()

    for u in range(3):
        for i in range(7):
            wait_all(st[u].at[pl.ds(0, 6), 0], near_r.at[u, i])
    for half in range(2):
        for e in range(1, NX):
            wait_all(stp.at[pl.ds(0, 6), 0, 0], pair_r.at[half, e])
    for way in range(2):
        for u in range(5):
            wait_all(sn[u].at[0] if u < OWN else snp.at[0, 0], next_r.at[way, u])

    def panel(s):
        h = cols_s[0, s] >> 3
        return rec[(z - (h >> 3) + NZ) & (NZ - 1), (x - ((h >> 1) & 3) + NX) & (NX - 1), (h & 1) ^ y]

    def row_step(i, before):
        s = tsm[0, i]
        row = rows_s[0, s]
        who = s >> 2
        tile = om[(yh - (who >> 1) + NH) & (NH - 1), who & 1, s & 3]
        prod = lax.dot_general(tile, panel(s), (((1,), (1,)), ((), ())), preferred_element_type=jnp.float32)
        total = jnp.where(row == before, acc[...], 0.0) + prod
        acc[...] = total
        yb[i] = total.astype(jnp.bfloat16)
        return row

    acc[...] = jnp.zeros_like(acc)
    lax.fori_loop(0, SLOTS, row_step, jnp.int32(-1), unroll=8)

    def grad(g, who, i):
        s = (((yh + g) % NH) * 2 + who) * 4 + i
        return jnp.dot(yb[tsm[1, s]], panel(s), preferred_element_type=jnp.float32)

    def for_pair(g):
        def one(i, carry):
            gx[g, i] = grad(g, 1 - core, i).astype(jnp.bfloat16)
            return carry

        lax.fori_loop(0, 4, one, 0, unroll=4)
        pair_copy(g).start()

    def for_me(g):
        def one(i, carry):
            gown[g, i] = grad(g, core, i)
            return carry

        lax.fori_loop(0, 4, one, 0, unroll=4)

    def pair_copy(g):
        return remote(gx.at[g], grx.at[g], gs.at[g], gr.at[g], cq)

    def half_copy(d):
        half = pl.ds(2 * d, 2)
        return remote(hs.at[half], relr.at[half], hss.at[d], hsr.at[d], hp if d == 0 else hm)

    def last_copy(d, h):
        half = pl.ds(2 * h, 2)
        return remote(fs.at[d, half], fr.at[d, half], fss.at[d, h], fsr.at[d, h], hp if d == 0 else hm)

    for_pair(2)
    for_me(2)
    for_pair(1)
    for_pair(3)
    pair_copy(2).wait_recv()
    hs[...] = (gown[2] + grx[2].astype(jnp.float32)).astype(jnp.bfloat16)
    half_copy(0).start()
    half_copy(1).start()
    for_me(1)
    for_me(3)
    for d, g in ((0, 1), (1, 3)):
        direct = 1 - d
        half = slice(2 * direct, 2 * direct + 2)
        pair_copy(g).wait_recv()
        fs[d, half] = (gown[g, half] + grx[g, half].astype(jnp.float32)).astype(jnp.bfloat16)
        last_copy(d, direct).start()
    for_pair(0)
    for_me(0)
    for d, g in ((0, 1), (1, 3)):
        half = slice(2 * d, 2 * d + 2)
        half_copy(d).wait_recv()
        fs[d, half] = (gown[g, half] + grx[g, half].astype(jnp.float32)
                       + relr[half].astype(jnp.float32)).astype(jnp.bfloat16)
        last_copy(d, d).start()
    pair_copy(0).wait_recv()
    for d in range(2):
        for h in range(2):
            last_copy(d, h).wait_recv()

    e0 = lax.broadcasted_iota(jnp.int32, (TILE, TILE), 0)
    e1 = lax.broadcasted_iota(jnp.int32, (TILE, TILE), 1)
    for i in range(4):
        s = t * 4 + i
        total = (gown[0, i] + grx[0, i].astype(jnp.float32)) + (fr[0, i].astype(jnp.float32) + fr[1, i].astype(jnp.float32))
        own = om[0, core, i].astype(jnp.float32)
        diag = jnp.where(rows_s[0, s] == cols_s[0, s], e0, -1) == e1
        inverse = jnp.where(diag, 1.0 / jnp.where(diag, own, 1.0), 0.0)
        stepped = own - 0.5 * (total / 2048.0 - inverse)
        shrunk = stepped - jnp.clip(stepped, -0.05, 0.05)
        out_ref[0, i] = jnp.where(diag, stepped, shrunk).astype(jnp.bfloat16)

    for dx, f in others:
        w_copy(dx, f).wait_send()
    gather_y.wait_send()
    table_up.wait_send()
    table_down.wait_send()
    for u in range(5):
        blocks = zb[u] if u < OWN else z2
        for way in range(2):
            if u in (1, 2, OTHER):
                z_copy(way, 1, u).wait_send()
            long = way == (0 if u < OWN else 1)
            wait_all(blocks.at[pl.ds(0, 2 if long else 1), pl.ds(0, 8)], zs.at[way, u])
    for d in range(2):
        om_copy(d, 0).wait_send()
        om_copy(d, 1).wait_send()
        half_copy(d).wait_send()
        for h in range(2):
            last_copy(d, h).wait_send()
    for g in range(4):
        om_core(g).wait_send()
        pair_copy(g).wait_send()
    for u in range(3):
        for i in range(7):
            wait_all(st[u].at[pl.ds(0, 6), 0], near_s.at[u, i])
    for half in range(2):
        for e in range(1, NX):
            wait_all(stp.at[pl.ds(0, 6), 0, 0], pair_s.at[half, e])
    for way in range(2):
        for u in range(5):
            wait_all(sn[u].at[0] if u < OWN else snp.at[0, 0], next_s.at[way, u])


def body(xdata, omega_tiles, tile_rows, tile_cols):
    bf, f32, i32 = jnp.bfloat16, jnp.float32, jnp.int32
    tile = (TILE, TILE)
    dma = pltpu.SemaphoreType.DMA
    vmem = pl.BlockSpec(memory_space=pltpu.VMEM)
    smem = pl.BlockSpec(memory_space=pltpu.SMEM)
    hbm = pl.BlockSpec(memory_space=pl.ANY)
    return pl.pallas_call(
        kernel,
        out_shape=jax.ShapeDtypeStruct(omega_tiles.shape, bf),
        in_specs=[hbm, hbm, vmem, vmem, smem, smem],
        out_specs=vmem,
        scratch_shapes=[
            *[pltpu.VMEM((NZ, 8, size, TILE), bf) for size in PARTS],
            pltpu.VMEM((NZ, 16, PAIR_ROWS, TILE), bf),
            *[pltpu.VMEM((NZ, 7, size, TILE), bf) for size in PARTS],
            pltpu.VMEM((NZ, 2, 3, PAIR_ROWS, TILE), bf),
            *[pltpu.VMEM((2, 8, size, TILE), bf) for size in PARTS],
            pltpu.VMEM((2, 2, NX, PAIR_ROWS, TILE), bf),
            pltpu.VMEM((NZ, NX, 2) + tile, bf),
            pltpu.VMEM((NH, 2, 4) + tile, bf),
            pltpu.VMEM((SLOTS,) + tile, bf),
            pltpu.VMEM(tile, f32),
            pltpu.VMEM((NH, 4) + tile, bf),
            pltpu.VMEM((NH, 4) + tile, bf),
            pltpu.VMEM((NH, 4) + tile, f32),
            pltpu.VMEM((4,) + tile, bf),
            pltpu.VMEM((4,) + tile, bf),
            pltpu.VMEM((2, 4) + tile, bf),
            pltpu.VMEM((2, 4) + tile, bf),
            pltpu.VMEM((9, 8, 128), i32),
            pltpu.VMEM((2, 8, 8, 128), i32),
            pltpu.SMEM((8, 8, 128), i32),
            pltpu.SMEM((2, 8, 8, 128), i32),
            pltpu.SMEM((8, 128), i32),
            dma((2, 5)), dma((2, 5)), dma((2, 4, 5)),
            dma((1,)), dma((1,)),
            dma((3, 7)), dma((3, 7)), dma((2, 4)), dma((2, 4)),
            dma((2, 5)), dma((2, 5)),
            dma((8,)), dma((8,)), dma((2,)), dma((2,)),
            dma((4,)), dma((4,)), dma((4,)), dma((4,)),
            dma((4,)), dma((4,)), dma((2,)), dma((2,)), dma((2, 2)), dma((2, 2)),
            dma((5, 8)),
        ],
        compiler_params=pltpu.CompilerParams(
            collective_id=0, has_side_effects=True, vmem_limit_bytes=60 * 1024 * 1024
        ),
    )(xdata, omega_tiles, tile_rows, tile_cols, tile_rows, tile_cols)


def solution(mesh):
    return jax.shard_map(
        body,
        mesh=mesh,
        in_specs=(P("team", "blk"), P("blk", "team", None, None), P("blk", None), P("blk", None)),
        out_specs=P("blk", "team", None, None),
        check_vma=False,
    )
```

```python
import jax
import jax.numpy as jnp
from jax import lax
from jax.experimental import pallas as pl
from jax.experimental.pallas import tpu as pltpu
from jax.sharding import PartitionSpec as P

MESH = pl.DeviceIdType.MESH
NZ, NX, NH = 8, 4, 4
TILE = 256
SLOTS = 32
PARTS = (64, 64, 48)
STARTS = (0, 64, 128)
PAIR_START, PAIR_ROWS = 176, 80
OWN, OTHER = 3, 4


def kernel(x_ref, om_ref, rows_v, cols_v, rows_s, cols_s, out_ref,
           zb0, zb1, zb2, z2, st0, st1, st2, stp, sn0, sn1, sn2, snp, rec, om, yb, acc, gx, grx, gown, hs, relr, fs, fr, wq, wqn, wsm, wsn, tsm,
           zs0, zs, zr, gys, gyr, near_s, near_r, pair_s, pair_r,
           next_s, next_r, wsend, wrecv, wns, wnr, oms, omr, ocs, ocr, gs, gr, hss, hsr, fss, fsr, loc):
    zb, st, sn = (zb0, zb1, zb2), (st0, st1, st2), (sn0, sn1, sn2)
    t = lax.axis_index("team")
    b = lax.axis_index("blk")
    core, yh = t % 2, t // 2
    z, x, y = b // 8, (b // 2) % 4, b % 2

    def plane(dx, f, dz=0):
        yy = 1 - y if f else y
        return (t, ((z + dz) % NZ) * 8 + ((x + dx) % NX) * 2 + yy)

    zp, zm = plane(0, 0, 1), plane(0, 0, NZ - 1)
    yq = plane(0, 1)
    cq = (yh * 2 + 1 - core, b)
    hp = (((yh + 1) % NH) * 2 + core, b)
    hm = (((yh + 3) % NH) * 2 + core, b)

    def remote(src, dst, ssem, rsem, dev):
        return pltpu.make_async_remote_copy(src_ref=src, dst_ref=dst, send_sem=ssem, recv_sem=rsem,
                                            device_id=dev, device_id_type=MESH)

    def wait_all(ref, sem):
        pltpu.make_async_copy(ref, ref, sem).wait()

    x_loads = []
    for c, (start, size) in enumerate(zip(STARTS + (PAIR_START,), PARTS + (PAIR_ROWS,))):
        x_loads.append([pltpu.make_async_copy(x_ref.at[pl.ds(start, size), pl.ds(j * TILE, TILE)],
                                              (zb[c] if c < OWN else z2).at[0, j], loc.at[c]) for j in range(8)])
    for c in (OWN, 0, 1, 2):
        for copy in x_loads[c]:
            copy.start()
    om_load = pltpu.make_async_copy(om_ref.at[0], om.at[0, core], loc.at[4])
    om_load.start()

    partners = [zp, zm, cq, hp, hm] + [plane(dx, f) for dx in range(NX) for f in range(2) if dx or f]
    barrier = pltpu.get_barrier_semaphore()
    for dev in partners:
        pl.semaphore_signal(barrier, inc=1, device_id=dev, device_id_type=MESH)

    i0 = lax.broadcasted_iota(jnp.int32, (SLOTS, SLOTS), 0)
    i1 = lax.broadcasted_iota(jnp.int32, (SLOTS, SLOTS), 1)
    eye = i0 == i1
    rb = jnp.broadcast_to(rows_v[...], (SLOTS, SLOTS))
    cb = jnp.broadcast_to(cols_v[...], (SLOTS, SLOTS))
    rc = jnp.broadcast_to(jnp.sum(jnp.where(eye, rb, 0), axis=1, keepdims=True), (SLOTS, SLOTS))
    cc = jnp.sum(jnp.where(eye, cb, 0), axis=1, keepdims=True)
    rank = jnp.sum(jnp.where((rb < rc) | ((rb == rc) & (i1 < i0)), 1, 0), axis=1, keepdims=True)
    order = jnp.sum(jnp.where(rank == i1, i0, 0), axis=0, keepdims=True)
    last = jnp.sum(jnp.where(rc <= rb, 1, 0), axis=0, keepdims=True) - 1
    lane = lax.broadcasted_iota(jnp.int32, (SLOTS, 128), 1)
    ccw = jnp.broadcast_to(cc, (SLOTS, 128))
    wanted = jnp.sum(jnp.where((ccw >> 3) == lane, ccw & 7, 0), axis=0, keepdims=True)
    wq[0] = jnp.broadcast_to(wanted, (8, 128))
    tsm_v = wq.at[8]
    tsm_v[0:1, 0:SLOTS] = order
    tsm_v[1:2, 0:SLOTS] = last

    pl.semaphore_wait(barrier, len(partners))

    def w_copy(dx, f):
        place = dx * 2 + f
        return remote(wq.at[0], wq.at[place], wsend.at[0], wrecv.at[0], plane(dx, f))

    others = [(dx, f) for dx in range(NX) for f in range(2) if dx or f]
    for dx, f in others:
        w_copy(dx, f).start()
    t_copy = pltpu.make_async_copy(wq.at[8], tsm, loc.at[5])
    t_copy.start()

    def z_ref(u, k):
        if u < OWN:
            return zb[u].at[k]
        return z2.at[k, pl.ds(0 if u == OWN else 8, 8)]

    def z_copy(d, k, u):
        send = (zs0 if k == 1 else zs).at[d, u]
        if d == 0:
            return remote(z_ref(u, k - 1), z_ref(u, k), send, zr.at[0, k - 1, u], zp)
        return remote(z_ref(u, (9 - k) % 8), z_ref(u, 8 - k), send, zr.at[1, k - 1, u], zm)

    gather_y = remote(z2.at[0, pl.ds(0, 8)], z2.at[0, pl.ds(8, 8)], gys.at[0], gyr.at[0], yq)

    def choose(e, f, k, other, panels, way=None):
        holder = ((z - k + NZ) % NZ) * 8 + x * 2 + (1 - y if other else y)
        place = ((NX - e) % NX) * 2 + f
        idx = wsm[place, 0, holder] if way is None else wsn[way, place, 0, holder]
        got = panels(0)
        for j in range(1, 8):
            got = jnp.where(idx == j, panels(j), got)
        return got

    def near_rows(u):
        return pl.ds(STARTS[u], PARTS[u])

    pair_rows = pl.ds(PAIR_START, PAIR_ROWS)

    def near_copy(u, k, i):
        e, f = others[i]
        return remote(st[u].at[k, i], rec.at[k, e, f, near_rows(u)], near_s.at[u], near_r.at[u], plane(e, f))

    def pair_copies(k, e, half):
        return remote(stp.at[k, half, e - 1], rec.at[k, e, half, pair_rows], pair_s.at[half], pair_r.at[half], plane(e, 0))

    def pick(u, k):
        if u < OWN:
            for i in (0, 2, 4, 6, 1, 3, 5):
                e, f = others[i]
                st[u][k, i] = choose(e, f, k, False, lambda j: zb[u][k, j])
                near_copy(u, k, i).start()
            rec[k, 0, 0, near_rows(u)] = choose(0, 0, k, False, lambda j: zb[u][k, j])
            return
        half = u - OWN
        for e in (2, 1, 3, 0):
            got = choose(e, 0, k, half == 1, lambda j: z2[k, 8 * half + j])
            if e == 0:
                rec[k, 0, half, pair_rows] = got
            else:
                stp[k, half, e - 1] = got
                pair_copies(k, e, half).start()

    def next_copy(u, k, way, e, f):
        dev = plane(e, f if u < OWN else 0, 1 if way == 0 else NZ - 1)
        there = rec.at[k + 1 if way == 0 else k - 1, e, f, near_rows(u) if u < OWN else pair_rows]
        here = sn[u].at[way, e * 2 + f] if u < OWN else snp.at[way, f, e]
        return remote(here, there, next_s.at[u], next_r.at[u], dev)

    def pick_next(u, k, way):
        for e in (2, 1, 3, 0):
            if u < OWN:
                for f in (1, 0):
                    sn[u][way, e * 2 + f] = choose(e, f, k, False, lambda j: zb[u][k, j], way)
                    next_copy(u, k, way, e, f).start()
            else:
                half = u - OWN
                snp[way, half, e] = choose(e, 0, k, half == 1, lambda j: z2[k, 8 * half + j], way)
                next_copy(u, k, way, e, half).start()

    def first_z(u):
        for way in range(2):
            z_copy(way, 1, u).start()

    for u in (OWN, 0, 1, 2):
        wait_all(z_ref(u, 0), loc.at[u])
        if u == OWN:
            gather_y.start()
        elif u != 2:
            first_z(u)

    om_load.wait()

    def om_copy(d, what):
        far = hp if d == 0 else hm
        if what == 0:
            return remote(om.at[0, core], om.at[1 if d == 0 else 3, core], oms.at[d], omr.at[d], far)
        half = pl.ds(0 if d == 0 else 2, 2)
        return remote(om.at[1 if d == 0 else 3, core, half], om.at[2, core, half], oms.at[2 + d], omr.at[2 + d], far)

    def om_core(g):
        return remote(om.at[g, core], om.at[g, core], ocs.at[g], ocr.at[g], cq)


    wait_all(wq.at[pl.ds(1, 7)], wrecv.at[0])
    w_load = pltpu.make_async_copy(wq.at[pl.ds(0, 8)], wsm, loc.at[6])
    w_load.start()
    table_up = remote(wq.at[pl.ds(0, 8)], wqn.at[1], wns.at[0], wnr.at[1], zp)
    table_down = remote(wq.at[pl.ds(0, 8)], wqn.at[0], wns.at[1], wnr.at[0], zm)
    table_up.start()
    table_down.start()
    w_load.wait()

    pick(0, 0)
    for way in range(2):
        z_copy(way, 1, 0).wait_send()
    first_z(2)
    pick(1, 0)
    for way in range(2):
        z_copy(way, 1, 1).wait_send()
    first_z(OWN)
    pick(2, 0)
    gather_y.wait_recv()
    first_z(OTHER)
    om_copy(0, 0).start()
    om_copy(1, 0).start()
    om_core(0).start()
    pick(OWN, 0)
    pick(OTHER, 0)

    for u in (0, 1, 2, OWN, OTHER):
        for way in range(2):
            z_copy(way, 1, u).wait_recv()
            z_copy(way, 2, u).start()
        pick(u, 1)
        pick(u, 7)

    table_up.wait_recv()
    table_down.wait_recv()
    n_load = pltpu.make_async_copy(wqn, wsn, loc.at[7])
    n_load.start()
    n_load.wait()

    for u in (0, 1, 2, OWN, OTHER):
        short = 1 if u < OWN else 0
        for way in range(2):
            z_copy(way, 2, u).wait_recv()
            if way != short:
                z_copy(way, 3, u).start()
            else:
                pick_next(u, 2 if way == 0 else 6, way)
        pick(u, 2)
        pick(u, 6)
        if u == 1:
            om_copy(0, 0).wait_recv()
            om_copy(0, 1).start()
            om_core(1).start()
            om_copy(1, 0).wait_recv()
            om_copy(1, 1).start()
            om_core(3).start()

    for u in (0, 1, 2, OWN, OTHER):
        way = 0 if u < OWN else 1
        z_copy(way, 3, u).wait_recv()
        pick_next(u, 3 if way == 0 else 5, way)
        pick(u, 3 if way == 0 else 5)

    om_copy(0, 1).wait_recv()
    om_copy(1, 1).wait_recv()
    om_core(2).start()
    t_copy.wait()
    for g in (0, 1, 3, 2):
        om_core(g).wait_recv()

    for u in range(3):
        wait_all(st[u].at[pl.ds(0, 6)], near_r.at[u])
    for half in range(2):
        wait_all(stp.at[pl.ds(0, 6), half], pair_r.at[half])
    for u in range(5):
        wait_all(sn[u] if u < OWN else snp.at[:, u - OWN], next_r.at[u])

    def panel(s):
        h = cols_s[0, s] >> 3
        return rec[(z - (h >> 3) + NZ) & (NZ - 1), (x - ((h >> 1) & 3) + NX) & (NX - 1), (h & 1) ^ y]

    def row_step(i, before):
        s = tsm[0, i]
        row = rows_s[0, s]
        who = s >> 2
        tile = om[(yh - (who >> 1) + NH) & (NH - 1), who & 1, s & 3]
        prod = lax.dot_general(tile, panel(s), (((1,), (1,)), ((), ())), preferred_element_type=jnp.float32)
        total = jnp.where(row == before, acc[...], 0.0) + prod
        acc[...] = total
        yb[i] = total.astype(jnp.bfloat16)
        return row

    acc[...] = jnp.zeros_like(acc)
    lax.fori_loop(0, SLOTS, row_step, jnp.int32(-1), unroll=8)

    def grad(g, who, i):
        s = (((yh + g) % NH) * 2 + who) * 4 + i
        return jnp.dot(yb[tsm[1, s]], panel(s), preferred_element_type=jnp.float32)

    def for_pair(g):
        def one(i, carry):
            gx[g, i] = grad(g, 1 - core, i).astype(jnp.bfloat16)
            return carry

        lax.fori_loop(0, 4, one, 0, unroll=4)
        pair_copy(g).start()

    def for_me(g):
        def one(i, carry):
            gown[g, i] = grad(g, core, i)
            return carry

        lax.fori_loop(0, 4, one, 0, unroll=4)

    def pair_copy(g):
        return remote(gx.at[g], grx.at[g], gs.at[g], gr.at[g], cq)

    def half_copy(d):
        half = pl.ds(2 * d, 2)
        return remote(hs.at[half], relr.at[half], hss.at[d], hsr.at[d], hp if d == 0 else hm)

    def last_copy(d, h):
        half = pl.ds(2 * h, 2)
        return remote(fs.at[d, half], fr.at[d, half], fss.at[d, h], fsr.at[d, h], hp if d == 0 else hm)

    for_pair(2)
    for_me(2)
    for_pair(1)
    for_pair(3)
    pair_copy(2).wait_recv()
    hs[...] = (gown[2] + grx[2].astype(jnp.float32)).astype(jnp.bfloat16)
    half_copy(0).start()
    half_copy(1).start()
    for_me(1)
    for_me(3)
    for d, g in ((0, 1), (1, 3)):
        direct = 1 - d
        half = slice(2 * direct, 2 * direct + 2)
        pair_copy(g).wait_recv()
        fs[d, half] = (gown[g, half] + grx[g, half].astype(jnp.float32)).astype(jnp.bfloat16)
        last_copy(d, direct).start()
    for_pair(0)
    for_me(0)
    for d, g in ((0, 1), (1, 3)):
        half = slice(2 * d, 2 * d + 2)
        half_copy(d).wait_recv()
        fs[d, half] = (gown[g, half] + grx[g, half].astype(jnp.float32)
                       + relr[half].astype(jnp.float32)).astype(jnp.bfloat16)
        last_copy(d, d).start()
    pair_copy(0).wait_recv()
    for d in range(2):
        for h in range(2):
            last_copy(d, h).wait_recv()

    e0 = lax.broadcasted_iota(jnp.int32, (TILE, TILE), 0)
    e1 = lax.broadcasted_iota(jnp.int32, (TILE, TILE), 1)
    for i in range(4):
        s = t * 4 + i
        total = (gown[0, i] + grx[0, i].astype(jnp.float32)) + (fr[0, i].astype(jnp.float32) + fr[1, i].astype(jnp.float32))
        own = om[0, core, i].astype(jnp.float32)
        diag = jnp.where(rows_s[0, s] == cols_s[0, s], e0, -1) == e1
        inverse = jnp.where(diag, 1.0 / jnp.where(diag, own, 1.0), 0.0)
        stepped = own - 0.5 * (total / 2048.0 - inverse)
        shrunk = stepped - jnp.clip(stepped, -0.05, 0.05)
        out_ref[0, i] = jnp.where(diag, stepped, shrunk).astype(jnp.bfloat16)

    wait_all(wq.at[pl.ds(1, 7)], wsend.at[0])
    gather_y.wait_send()
    table_up.wait_send()
    table_down.wait_send()
    for u in range(5):
        blocks = zb[u] if u < OWN else z2
        for way in range(2):
            if u in (2, OWN, OTHER):
                z_copy(way, 1, u).wait_send()
            long = way == (0 if u < OWN else 1)
            wait_all(blocks.at[pl.ds(0, 2 if long else 1), pl.ds(0, 8)], zs.at[way, u])
    for d in range(2):
        om_copy(d, 0).wait_send()
        om_copy(d, 1).wait_send()
        half_copy(d).wait_send()
        for h in range(2):
            last_copy(d, h).wait_send()
    for g in range(4):
        om_core(g).wait_send()
        pair_copy(g).wait_send()
    for u in range(3):
        wait_all(st[u].at[pl.ds(0, 6)], near_s.at[u])
    for half in range(2):
        wait_all(stp.at[pl.ds(0, 6), half], pair_s.at[half])
    for u in range(5):
        wait_all(sn[u] if u < OWN else snp.at[:, u - OWN], next_s.at[u])


def body(xdata, omega_tiles, tile_rows, tile_cols):
    bf, f32, i32 = jnp.bfloat16, jnp.float32, jnp.int32
    tile = (TILE, TILE)
    dma = pltpu.SemaphoreType.DMA
    vmem = pl.BlockSpec(memory_space=pltpu.VMEM)
    smem = pl.BlockSpec(memory_space=pltpu.SMEM)
    hbm = pl.BlockSpec(memory_space=pl.ANY)
    return pl.pallas_call(
        kernel,
        out_shape=jax.ShapeDtypeStruct(omega_tiles.shape, bf),
        in_specs=[hbm, hbm, vmem, vmem, smem, smem],
        out_specs=vmem,
        scratch_shapes=[
            *[pltpu.VMEM((NZ, 8, size, TILE), bf) for size in PARTS],
            pltpu.VMEM((NZ, 16, PAIR_ROWS, TILE), bf),
            *[pltpu.VMEM((NZ, 7, size, TILE), bf) for size in PARTS],
            pltpu.VMEM((NZ, 2, 3, PAIR_ROWS, TILE), bf),
            *[pltpu.VMEM((2, 8, size, TILE), bf) for size in PARTS],
            pltpu.VMEM((2, 2, NX, PAIR_ROWS, TILE), bf),
            pltpu.VMEM((NZ, NX, 2) + tile, bf),
            pltpu.VMEM((NH, 2, 4) + tile, bf),
            pltpu.VMEM((SLOTS,) + tile, bf),
            pltpu.VMEM(tile, f32),
            pltpu.VMEM((NH, 4) + tile, bf),
            pltpu.VMEM((NH, 4) + tile, bf),
            pltpu.VMEM((NH, 4) + tile, f32),
            pltpu.VMEM((4,) + tile, bf),
            pltpu.VMEM((4,) + tile, bf),
            pltpu.VMEM((2, 4) + tile, bf),
            pltpu.VMEM((2, 4) + tile, bf),
            pltpu.VMEM((9, 8, 128), i32),
            pltpu.VMEM((2, 8, 8, 128), i32),
            pltpu.SMEM((8, 8, 128), i32),
            pltpu.SMEM((2, 8, 8, 128), i32),
            pltpu.SMEM((8, 128), i32),
            dma((2, 5)), dma((2, 5)), dma((2, 3, 5)),
            dma((1,)), dma((1,)),
            dma((3,)), dma((3,)), dma((2,)), dma((2,)),
            dma((5,)), dma((5,)),
            dma((1,)), dma((1,)), dma((2,)), dma((2,)),
            dma((4,)), dma((4,)), dma((4,)), dma((4,)),
            dma((4,)), dma((4,)), dma((2,)), dma((2,)), dma((2, 2)), dma((2, 2)),
            dma((8,)),
        ],
        compiler_params=pltpu.CompilerParams(
            collective_id=0, has_side_effects=True, vmem_limit_bytes=60 * 1024 * 1024
        ),
    )(xdata, omega_tiles, tile_rows, tile_cols, tile_rows, tile_cols)


def solution(mesh):
    return jax.shard_map(
        body,
        mesh=mesh,
        in_specs=(P("team", "blk"), P("blk", "team", None, None), P("blk", None), P("blk", None)),
        out_specs=P("blk", "team", None, None),
        check_vma=False,
    )
```
